128 devices in a mesh: section: 4 (over z_hi, core), space: 32 (over z_lo, y, x).
Axes of the slice: x: 4, y: 4, z: 4 (z_hi: 2, z_lo: 2; z = z_hi * 2 + z_lo), core: 2. Of those that a mesh axis runs over, the one named last changes fastest.
Arguments:
- carried: float32 [2, 3, 2, 4, 64, 512], P(None, None, None, None, 'space'), may hold values from -6 to 6
- source_field: float32 [2, 3, 2, 4, 64, 512], P(None, None, None, None, 'space'), may hold values from -6 to 6
- source_slice: int32 [4], replicated, may hold values from 0 to 3, as said below
- space_links: float32 [4, 3, 2, 3, 3, 64, 512], P('section', None, None, None, None, 'space'), may hold values from -2.5 to 2.5
- time_links: float32 [4, 2, 3, 3, 64, 512], P('section', None, None, None, 'space'), may hold values from -2.5 to 2.5
- magnetic: float32 [4, 3, 2, 3, 3, 64, 512], P('section', None, None, None, None, 'space'), may hold values from -4 to 4
Outputs:
- smeared: float32 [4, 2, 3, 2, 4, 64, 512], P('section', None, None, None, None, 'space')
The draws below stay inside these ranges and needn't reach their ends.
Inputs may be any that keep to these rules, and one draw needn't show every extreme that they name: `source_slice`: every group number from 0 to 3 occurs among the columns.
All inputs are finite; a program needn't handle non-finite values.
Results may differ from the reference program's by a relative error of at most 0.00002.
Values sent between devices are 32-bit elements; how exact they have to be, the bound alone decides.
No kernel may reach another device: no remote copies, remote signals or barrier semaphores. Data moves between devices by JAX's collectives and lax.ppermute only.
A program may use at most 128 MiB of HBM per device.

```python
import jax
import jax.numpy as jnp

LY = 32
LZ = 16
COLS = 4
SMEAR = 2
X = 64
N_SECTION = 4


def draw_source_slice(key, part):
    key = jax.random.fold_in(key, 11)
    return jax.random.permutation(key, jnp.arange(COLS) % N_SECTION).astype(jnp.int32)


def steps_of(own_key, dims, pieces, least, high):
    def one(axis_at, parts):
        draws = jax.random.uniform(jax.random.fold_in(jax.random.fold_in(own_key, 6), axis_at), (parts,), jnp.float32, least / len(pieces), high / len(pieces))
        return jnp.repeat(jnp.exp(draws), dims[axis_at] // parts).reshape((-1,) + (1,) * (len(dims) - axis_at - 1))

    level = one(*pieces[0])
    for cut in pieces[1:]:
        level = level * one(*cut)
    return level


def centred(own_key, shape, deviation, most, pieces=(), kind=jnp.bfloat16):
    array = jax.random.normal(own_key, shape, jnp.float32) * deviation
    if len(pieces) > 0:
        array = steps_of(own_key, shape, pieces, -0.22, 0.18) * array
    return jnp.clip(array, min=-most, max=most).astype(kind)


def setup_inputs(seed: int = 0) -> dict:
    seeds = jax.random.split(jax.random.key(seed), 7)
    carried = centred(seeds[0], (2, 3, 2, COLS, X, LY * LZ), 1.0, 6.0, ((4, 32),), jnp.float32)
    source_field = centred(seeds[1], (2, 3, 2, COLS, X, LY * LZ), 1.0, 6.0, ((4, 32),), jnp.float32)
    source_slice = draw_source_slice(jax.random.fold_in(seeds[6], 71), 0)
    space_links = centred(seeds[3], (N_SECTION, 3, 2, 3, 3, X, LY * LZ), 6 ** -0.5, 2.5, ((0, 4), (5, 32)), jnp.float32)
    time_links = centred(seeds[4], (N_SECTION, 2, 3, 3, X, LY * LZ), 6 ** -0.5, 2.5, ((0, 4), (4, 32)), jnp.float32)
    magnetic = centred(seeds[5], (N_SECTION, 3, 2, 3, 3, X, LY * LZ), 0.6, 4.0, ((0, 4), (5, 32)), jnp.float32)
    return {"carried": carried, "source_field": source_field, "source_slice": source_slice, "space_links": space_links, "time_links": time_links, "magnetic": magnetic}


KINETIC = 1.0 / 6.0
QUARTIC = 1.0 / 216.0
SPIN_WEIGHT = 1.0 / 6.0
SMEAR_WEIGHT = 0.1


def colour_product(link, field, dagger):
    parts_real = []
    parts_imag = []
    for colour_out in range(3):
        sum_real = 0.0
        sum_imag = 0.0
        for colour_in in range(3):
            if dagger:
                link_real = link[0, colour_in, colour_out]
                link_imag = -link[1, colour_in, colour_out]
            else:
                link_real = link[0, colour_out, colour_in]
                link_imag = link[1, colour_out, colour_in]
            field_real = field[0, colour_in]
            field_imag = field[1, colour_in]
            sum_real = sum_real + link_real * field_real - link_imag * field_imag
            sum_imag = sum_imag + link_real * field_imag + link_imag * field_real
        parts_real.append(sum_real)
        parts_imag.append(sum_imag)
    return jnp.stack([jnp.stack(parts_real), jnp.stack(parts_imag)])


def depth_forward(field):
    depth_index = jnp.arange(field.shape[-1]) % LZ
    return jnp.where(depth_index < LZ - 1, jnp.roll(field, -1, -1), jnp.roll(field, LZ - 1, -1))


def depth_backward(field):
    depth_index = jnp.arange(field.shape[-1]) % LZ
    return jnp.where(depth_index > 0, jnp.roll(field, 1, -1), jnp.roll(field, -(LZ - 1), -1))


def laplace(padded, links_near):
    core = padded[..., 1:-1, :]
    inner = links_near[..., 1:-1, :]
    total = colour_product(inner[0], padded[..., 2:, :], False)
    total = total + colour_product(links_near[0][..., :-2, :], padded[..., :-2, :], True)
    total = total + colour_product(inner[1], jnp.roll(core, -LZ, -1), False)
    total = total + jnp.roll(colour_product(inner[1], core, True), LZ, -1)
    total = total + colour_product(inner[2], depth_forward(core), False)
    total = total + depth_backward(colour_product(inner[2], core, True))
    return total - 6.0 * core


def links_within(padded_links, extent):
    offset = (padded_links.shape[-2] - extent) // 2
    return padded_links[..., offset:offset + extent, :]


def periodic_pad(field, width):
    return jnp.concatenate([field[..., -width:, :], field, field[..., :width, :]], axis=-2)


def hermitian(raw):
    real_part = 0.5 * (raw[:, 0] + jnp.swapaxes(raw[:, 0], 1, 2))
    imag_part = 0.5 * (raw[:, 1] - jnp.swapaxes(raw[:, 1], 1, 2))
    return jnp.stack([real_part, imag_part], axis=1)


def times_minus_i(value):
    return jnp.stack([value[1], -value[0]])


def times_plus_i(value):
    return jnp.stack([-value[1], value[0]])


def spin_field(colour_field, spinor):
    spin_up = spinor[:, :, 0]
    spin_down = spinor[:, :, 1]
    upper = colour_product(colour_field[0], spin_down, False)
    upper = upper + times_minus_i(colour_product(colour_field[1], spin_down, False))
    upper = upper + colour_product(colour_field[2], spin_up, False)
    lower = colour_product(colour_field[0], spin_up, False)
    lower = lower + times_plus_i(colour_product(colour_field[1], spin_up, False))
    lower = lower - colour_product(colour_field[2], spin_down, False)
    return jnp.stack([upper, lower], axis=2)


def step_a(spinor, padded_links, colour_field):
    padded = periodic_pad(spinor, 1)
    single = laplace(padded, links_within(padded_links, padded.shape[-2]))
    padded = periodic_pad(single, 1)
    double = laplace(padded, links_within(padded_links, padded.shape[-2]))
    hamiltonian = -KINETIC * single - QUARTIC * double - SPIN_WEIGHT * spin_field(colour_field, spinor)
    return spinor - 0.5 * hamiltonian


def reference(carried, source_field, source_slice, space_links, time_links, magnetic):
    holding = carried
    finished = []
    for group in range(N_SECTION):
        padded_links = periodic_pad(space_links[group], max(2, SMEAR))
        colour_field = hermitian(magnetic[group])
        halfway = step_a(holding, padded_links, colour_field)
        rotated = colour_product(time_links[group], halfway, True)
        injected = (source_slice == group).astype(jnp.float32).reshape(1, 1, 1, -1, 1, 1)
        holding = step_a(rotated, padded_links, colour_field) + injected * source_field
        spinor = holding
        for sweep in range(SMEAR):
            padded = periodic_pad(spinor, 1)
            spinor = spinor + SMEAR_WEIGHT * laplace(padded, links_within(padded_links, padded.shape[-2]))
        finished.append(spinor)
    return jnp.stack(finished)
```

```python
import jax
import jax.numpy as jnp
from jax import lax
from jax.experimental import pallas as pl
from jax.experimental.pallas import tpu as pltpu
from jax.sharding import PartitionSpec as P


LZ = 16
KINETIC = 1.0 / 6.0
QUARTIC = 1.0 / 216.0
SPIN_WEIGHT = 1.0 / 6.0
SMEAR_WEIGHT = 0.1
AXES = ("section", "space")
VMEM = pltpu.VMEM
PATH = (
    (1, 0), (0, 0), (0, 1), (1, 1), (1, 2), (0, 2), (0, 3), (1, 3),
    (2, 3), (3, 3), (3, 2), (2, 2), (2, 1), (3, 1), (3, 0), (2, 0),
)
BLOCKS = len(PATH)


def place(half, ring, block, core):
    x, y = PATH[block % BLOCKS]
    return (2 * half + core) * 32 + ring * 16 + y * 4 + x


def natural(half, turn, pair):
    return (2 * half + turn) * 32 + pair


def every():
    return [
        (half, ring, block, core)
        for half in range(2)
        for ring in range(2)
        for block in range(BLOCKS)
        for core in range(2)
    ]


def across():
    return [
        (place(h, r, m, c), place(h, r, m + 1, 0) if c else place(h, r, m - 1, 1))
        for h, r, m, c in every()
    ]


def sibling():
    return [(place(h, r, m, c), place(h, r, m, 1 - c)) for h, r, m, c in every()]


def onward():
    return [(place(h, r, m, c), place(1 - h, r, m, c)) for h, r, m, c in every()]


def spread(way):
    return [
        (natural(h, r ^ way, 2 * m + c), place(h, r, m, c)) for h, r, m, c in every()
    ]


def collect(way):
    return [(there, here) for here, there in spread(way)]


def rows_of(shape):
    return lax.broadcasted_iota(jnp.int32, shape, len(shape) - 2)


def lanes_of(shape):
    return lax.broadcasted_iota(jnp.int32, shape, len(shape) - 1)


def roll(value, by, axis):
    return pltpu.roll(value, by, value.ndim + axis)


def swap_planes(value):
    first = rows_of(value.shape) % 2 == 0
    return jnp.where(first, roll(value, 7, -2), roll(value, 1, -2))


def y_forward(value):
    moved = roll(value, 112, -1)
    return jnp.where(lanes_of(value.shape) < 112, moved, roll(moved, 6, -2))


def y_backward(value):
    moved = roll(value, 16, -1)
    return jnp.where(lanes_of(value.shape) >= 16, moved, roll(moved, 2, -2))


def z_forward(value):
    inside = lanes_of(value.shape) % LZ < LZ - 1
    return jnp.where(inside, roll(value, 127, -1), roll(value, LZ - 1, -1))


def z_backward(value):
    inside = lanes_of(value.shape) % LZ > 0
    return jnp.where(inside, roll(value, 1, -1), roll(value, 129 - LZ, -1))


def add(one, other):
    return [a + b for a, b in zip(one, other)]


def scaled(factor, field):
    return [factor * a for a in field]


def link_at(ref, base):
    def entry(row, column):
        return ref[base + 3 * row + column], ref[base + 9 + 3 * row + column]

    return entry


def product(entry, field, dagger, total=None):
    real, imag = [], []
    for out in range(3):
        sum_real = None if total is None else total[out]
        sum_imag = None if total is None else total[3 + out]
        for inner in range(3):
            link_real, link_imag = entry(inner, out) if dagger else entry(out, inner)
            field_real, field_imag = field[inner], field[3 + inner]
            cross_real, cross_imag = link_imag * field_imag, link_imag * field_real
            part_real, part_imag = link_real * field_real, link_real * field_imag
            if dagger:
                part_real, part_imag = part_real + cross_real, part_imag - cross_imag
            else:
                part_real, part_imag = part_real - cross_real, part_imag + cross_imag
            sum_real = part_real if sum_real is None else sum_real + part_real
            sum_imag = part_imag if sum_imag is None else sum_imag + part_imag
        real.append(sum_real)
        imag.append(sum_imag)
    return real + imag


INNER, ALONG_Y, ALONG_Z = 0, 18, 36


def within(links, field):
    total = scaled(-6.0, field)
    total = product(link_at(links, ALONG_Y), [y_forward(a) for a in field], False, total)
    back = product(link_at(links, ALONG_Y), field, True)
    total = add(total, [y_backward(a) for a in back])
    total = product(link_at(links, ALONG_Z), [z_forward(a) for a in field], False, total)
    back = product(link_at(links, ALONG_Z), field, True)
    total = add(total, [z_backward(a) for a in back])
    return product(link_at(links, INNER), [swap_planes(a) for a in field], False, total)


LADDER, LEVEL, TIME = 0, 18, 27


def level_entry(ref):
    def entry(row, column):
        if row == column:
            return ref[LEVEL + row], None
        slot = min(row, column) + max(row, column) - 1
        imag = ref[LEVEL + 6 + slot]
        return ref[LEVEL + 3 + slot], imag if row < column else -imag

    return entry


def hermitian_product(entry, field):
    real, imag = [], []
    for out in range(3):
        sum_real = sum_imag = None
        for inner in range(3):
            link_real, link_imag = entry(out, inner)
            part_real, part_imag = link_real * field[inner], link_real * field[3 + inner]
            if link_imag is not None:
                part_real = part_real - link_imag * field[3 + inner]
                part_imag = part_imag + link_imag * field[inner]
            sum_real = part_real if sum_real is None else sum_real + part_real
            sum_imag = part_imag if sum_imag is None else sum_imag + part_imag
        real.append(sum_real)
        imag.append(sum_imag)
    return real + imag


def spin_term(others, field):
    up, down = [a[0] for a in field], [a[1] for a in field]
    ladder, level = link_at(others, LADDER), level_entry(others)
    upper = add(hermitian_product(level, up), product(ladder, down, False))
    lower = product(ladder, up, True)
    lower = [a - b for a, b in zip(lower, hermitian_product(level, down))]
    return [jnp.stack([a, b]) for a, b in zip(upper, lower)]


def load(ref, column):
    return [ref[column, part] for part in range(6)]


def store(ref, column, field):
    for part in range(6):
        ref[column, part] = field[part]


def prepare(field, links, own_side, partial_ref, across_ref, sibling_ref, column):
    partial = within(links, field)
    store(partial_ref, column, partial)
    for part in range(6):
        turned = swap_planes(partial[part])
        across_ref[column, part] = jnp.where(own_side, field[part], turned)
        sibling_ref[column, part] = jnp.where(own_side, turned, field[part])


def two_laplacians(field, partial, from_across, from_sibling, links, outer, own_side):
    beyond = [
        swap_planes(jnp.where(own_side, s, a)) for a, s in zip(from_across, from_sibling)
    ]
    rim = [jnp.where(own_side, a, s) for a, s in zip(from_across, from_sibling)]
    single = product(link_at(outer, 0), beyond, False, partial)
    rim = product(link_at(outer, 0), field, True, rim)
    double = product(link_at(outer, 0), rim, False, within(links, single))
    return single, double


def kernel_call(body, inputs, outputs, pinned=True):
    if pinned:
        inputs = [pltpu.with_memory_space_constraint(value, VMEM) for value in inputs]
    spec = pl.BlockSpec(memory_space=VMEM)
    shapes = [VMEM(shape, jnp.float32) for shape in outputs]
    return pl.pallas_call(
        body,
        in_specs=[spec] * len(inputs),
        out_specs=[spec] * len(outputs),
        out_shape=shapes,
        compiler_params=pltpu.CompilerParams(vmem_limit_bytes=32 * 1024 * 1024),
    )(*inputs)


FIELD = (2, 6, 2, 8, 128)
SIDE, RING, HALF = 0, 1, 2


def first_message(carried, space, marks, message):
    core = marks[RING] > 0
    message[pl.ds(0, 54)] = space[...]
    for column in range(2):
        for part in range(6):
            for spin in range(2):
                picked = jnp.where(core, carried[part, spin, 2 + column], carried[part, spin, column])
                message[54 + column * 12 + part * 2 + spin] = picked


def second_message(source, magnetic, time, marks, message):
    core = marks[RING] > 0

    def raw(axis, imag, row, column):
        return magnetic[axis * 18 + imag * 9 + row * 3 + column]

    def real(axis, row, column):
        return 0.5 * (raw(axis, 0, row, column) + raw(axis, 0, column, row))

    def imag(axis, row, column):
        return 0.5 * (raw(axis, 1, row, column) - raw(axis, 1, column, row))

    for row in range(3):
        for column in range(3):
            at = LADDER + 3 * row + column
            message[at] = real(0, row, column) + imag(1, row, column)
            message[at + 9] = imag(0, row, column) - real(1, row, column)
        message[LEVEL + row] = real(2, row, row)
    for slot, (row, column) in enumerate(((0, 1), (0, 2), (1, 2))):
        message[LEVEL + 3 + slot] = real(2, row, column)
        message[LEVEL + 6 + slot] = imag(2, row, column)
    message[pl.ds(TIME, 18)] = time[...]
    for column in range(2):
        for part in range(6):
            for spin in range(2):
                picked = jnp.where(core, source[part, spin, 2 + column], source[part, spin, column])
                message[45 + column * 12 + part * 2 + spin] = picked


def arrange(got0, got1, marks, field, links_a, links_b, plain_a, plain_b, partial, to_across, to_sibling):
    ring = marks[RING] > 0
    own_side = marks[SIDE] > 0
    first = rows_of((8, 128)) % 2 == 0
    for turn, links, plain in ((0, links_a, plain_a), (1, links_b, plain_b)):
        for at in range(18, 54):
            one, other = (got0[at], got1[at]) if turn == 0 else (got1[at], got0[at])
            links[at] = jnp.where(ring, other, one)
        for at in range(18):
            one, other = (got0[at], got1[at]) if turn == 0 else (got1[at], got0[at])
            plain[at] = jnp.where(ring, other, one)
        for row in range(3):
            for column in range(3):
                at, turned = 3 * row + column, 3 * column + row
                links[at] = jnp.where(first, plain[at], swap_planes(plain[turned]))
                links[at + 9] = jnp.where(first, plain[at + 9], -swap_planes(plain[turned + 9]))
        for at in range(9):
            edge = jnp.where(first, swap_planes(plain[at + 9]), plain[at])
            to_across[24 + 9 * turn + at] = edge
            to_sibling[24 + 9 * turn + at] = edge

    def one_column(column, carry):
        values = [got0[pl.ds(54 + column * 12 + part * 2, 2)] for part in range(6)]
        store(field, column, values)
        total = within(links_a, values)
        store(partial, column, total)
        for part in range(6):
            turned = swap_planes(total[part])
            to_across[pl.ds(column * 12 + part * 2, 2)] = jnp.where(own_side, values[part], turned)
            to_sibling[pl.ds(column * 12 + part * 2, 2)] = jnp.where(own_side, turned, values[part])
        return carry

    lax.fori_loop(0, 2, one_column, 0)


def edges(from_across, from_sibling, plain_a, plain_b, got0, got1, marks, outer_a, outer_b, others_a, others_b):
    own_side = marks[SIDE] > 0
    ring = marks[RING] > 0
    first = rows_of((8, 128)) % 2 == 0
    upper_core = jnp.logical_xor(own_side, first)
    for turn, plain, outer in ((0, plain_a, outer_a), (1, plain_b, outer_b)):
        for row in range(3):
            for column in range(3):
                at, turned = 3 * row + column, 24 + 9 * turn + 3 * column + row
                edge = jnp.where(upper_core, from_sibling[turned], from_across[turned])
                outer[at] = jnp.where(first, swap_planes(edge), plain[at])
                outer[at + 9] = jnp.where(first, -edge, plain[at + 9])
    for at in range(45):
        others_a[at] = jnp.where(ring, got1[at], got0[at])
        others_b[at] = jnp.where(ring, got0[at], got1[at])


def step_a(field, partial, from_across, from_sibling, links, outer, others, own_side):
    single, double = two_laplacians(field, partial, from_across, from_sibling, links, outer, own_side)
    spin = spin_term(others, field)
    return [
        f + (0.5 * KINETIC) * s + (0.5 * QUARTIC) * d + (0.5 * SPIN_WEIGHT) * b
        for f, s, d, b in zip(field, single, double, spin)
    ]


def first_half(field, partial, from_across, from_sibling, links, outer, others, marks, *outs):
    turned_field, *messages = outs
    own_side = marks[SIDE] > 0

    def one_column(column, carry):
        values = step_a(
            load(field, column), load(partial, column), load(from_across, column),
            load(from_sibling, column), links, outer, others, own_side,
        )
        values = product(link_at(others, TIME), values, True)
        store(turned_field, column, values)
        prepare(values, links, own_side, *messages, column)
        return carry

    lax.fori_loop(0, 2, one_column, 0)


def second_half(field, partial, from_across, from_sibling, links, outer, others, source, marks, *rest):
    *after, result = rest[:-3] if len(rest) > 1 else rest
    messages = rest[-3:] if len(rest) > 1 else None
    own_side = marks[SIDE] > 0

    def one_column(column, carry):
        values = step_a(
            load(field, column), load(partial, column), load(from_across, column),
            load(from_sibling, column), links, outer, others, own_side,
        )
        values = add(values, load(source, column))
        store(result, column, values)
        if messages is not None:
            prepare(values, after[0], own_side, *messages, column)
        return carry

    lax.fori_loop(0, 2, one_column, 0)


def only_prepare(field, links, marks, *messages):
    own_side = marks[SIDE] > 0

    def one_column(column, carry):
        prepare(load(field, column), links, own_side, *messages, column)
        return carry

    lax.fori_loop(0, 2, one_column, 0)


def smear_start(early_a, early_b, late_a, late_b, links_a, links_b, marks, field_a, field_b, *messages):
    own_side = marks[SIDE] > 0
    half = marks[HALF] > 0
    for turn, early, late, links, field in (
        (0, early_a, late_a, links_a, field_a),
        (1, early_b, late_b, links_b, field_b),
    ):

        def one_column(column, carry):
            values = [jnp.where(half, b, a) for a, b in zip(load(early, column), load(late, column))]
            store(field, column, values)
            prepare(values, links, own_side, *[ref.at[turn] for ref in messages], column)
            return carry

        lax.fori_loop(0, 2, one_column, 0)


def smear_end(field_a, field_b, partial, from_across, from_sibling, links_a, links_b, outer_a, outer_b, marks, out0, out1):
    own_side = marks[SIDE] > 0
    ring = marks[RING] > 0

    def smeared(turn, field_ref, links, outer, column):
        field = load(field_ref, column)
        single, double = two_laplacians(
            field, load(partial.at[turn], column), load(from_across.at[turn], column),
            load(from_sibling.at[turn], column), links, outer, own_side,
        )
        return [
            f + (2 * SMEAR_WEIGHT) * s + (SMEAR_WEIGHT * SMEAR_WEIGHT) * d
            for f, s, d in zip(field, single, double)
        ]

    def one_column(column, carry):
        one = smeared(0, field_a, links_a, outer_a, column)
        other = smeared(1, field_b, links_b, outer_b, column)
        store(out0, column, [jnp.where(ring, b, a) for a, b in zip(one, other)])
        store(out1, column, [jnp.where(ring, a, b) for a, b in zip(one, other)])
        return carry

    lax.fori_loop(0, 2, one_column, 0)


def deliver(got0, got1, marks, out):
    core = marks[RING] > 0
    for column in range(2):
        for part in range(6):
            for spin in range(2):
                one, other = got0[column, part, spin], got1[column, part, spin]
                out[part, spin, column] = jnp.where(core, other, one)
                out[part, spin, 2 + column] = jnp.where(core, one, other)


def registers(value, lead):
    rows = value.reshape(lead + (2, 4, 128))
    return jnp.swapaxes(rows, -3, -2).reshape(lead + (8, 128))


def exchange(to_across, to_sibling):
    return lax.ppermute(to_across, AXES, across()), lax.ppermute(to_sibling, AXES, sibling())


def full(flag):
    return jnp.broadcast_to(flag.astype(jnp.float32), (8, 128))


def local(carried, source_field, source_slice, space_links, time_links, magnetic):
    section, space = lax.axis_index("section"), lax.axis_index("space")
    core, half, ring = section % 2, section // 2, space // 16
    first = (jnp.arange(8) % 2)[:, None] == core
    side = jnp.broadcast_to(first.astype(jnp.float32), (8, 128))
    marks = jnp.stack([side, full(ring == 1), full(half == 1)])
    core_marks = jnp.stack([side, full(core == 1), full(half == 1)])

    carried = registers(carried, (6, 2, 4))
    source_field = registers(source_field, (6, 2, 4))
    space_links = registers(space_links, (54,))
    time_links = registers(time_links, (18,))
    magnetic = registers(magnetic, (54,))

    (message,) = kernel_call(first_message, [carried, space_links, core_marks], [(78, 8, 128)], False)
    got0 = lax.ppermute(message, AXES, spread(0))
    got1 = lax.ppermute(message[:54], AXES, spread(1))
    (message,) = kernel_call(
        second_message, [source_field, magnetic, time_links, core_marks], [(69, 8, 128)], False
    )
    more0 = lax.ppermute(message, AXES, spread(0))
    more1 = lax.ppermute(message[:45], AXES, spread(1))

    field, links_a, links_b, plain_a, plain_b, partial, to_across, to_sibling = kernel_call(
        arrange,
        [got0, got1, marks],
        [FIELD, (54, 8, 128), (54, 8, 128), (18, 8, 128), (18, 8, 128), FIELD, (42, 8, 128), (42, 8, 128)],
    )
    from_across, from_sibling = exchange(to_across, to_sibling)
    outer_a, outer_b, others_a, others_b = kernel_call(
        edges,
        [from_across, from_sibling, plain_a, plain_b, more0, more1, marks],
        [(18, 8, 128), (18, 8, 128), (45, 8, 128), (45, 8, 128)],
    )
    from_across = from_across[:24].reshape(FIELD)
    from_sibling = from_sibling[:24].reshape(FIELD)
    source = more0[45:].reshape(FIELD)
    here = lax.dynamic_slice_in_dim(source_slice, 2 * ring, 2)
    sources = [
        jnp.where(here == 2 * half + turn, 1.0, 0.0).astype(jnp.float32).reshape(2, 1, 1, 1, 1) * source
        for turn in range(2)
    ]
    links, outer, others = (links_a, links_b), (outer_a, outer_b), (others_a, others_b)
    results = []
    for phase in range(2):
        for turn in range(2):
            field, partial, to_across, to_sibling = kernel_call(
                first_half,
                [field, partial, from_across, from_sibling, links[turn], outer[turn], others[turn], marks],
                [FIELD] * 4,
            )
            from_across, from_sibling = exchange(to_across, to_sibling)
            inputs = [field, partial, from_across, from_sibling, links[turn], outer[turn], others[turn]]
            inputs += [sources[turn], marks]
            if turn == 0:
                field, partial, to_across, to_sibling = kernel_call(
                    second_half, inputs + [links[1]], [FIELD] * 4
                )
                from_across, from_sibling = exchange(to_across, to_sibling)
            else:
                (field,) = kernel_call(second_half, inputs, [FIELD])
            results.append(field)
        if phase == 0:
            field = lax.ppermute(field, AXES, onward())
            partial, to_across, to_sibling = kernel_call(
                only_prepare, [field, links_a, marks], [FIELD] * 3
            )
            from_across, from_sibling = exchange(to_across, to_sibling)

    both = (2,) + FIELD
    field_a, field_b, partial, to_across, to_sibling = kernel_call(
        smear_start, results + [links_a, links_b, marks], [FIELD, FIELD, both, both, both]
    )
    from_across, from_sibling = exchange(to_across, to_sibling)
    out0, out1 = kernel_call(
        smear_end,
        [field_a, field_b, partial, from_across, from_sibling, links_a, links_b, outer_a, outer_b, marks],
        [FIELD, FIELD],
    )
    out0 = lax.ppermute(out0, AXES, collect(0))
    out1 = lax.ppermute(out1, AXES, collect(1))
    (out,) = kernel_call(deliver, [out0, out1, core_marks], [(6, 2, 4, 8, 128)])
    out = jnp.swapaxes(out.reshape(2, 3, 2, 4, 4, 2, 128), -3, -2)
    return out.reshape(1, 2, 3, 2, 4, 2, 512)


def solution(mesh):
    return jax.shard_map(
        local,
        mesh=mesh,
        in_specs=(
            P(None, None, None, None, "space", None),
            P(None, None, None, None, "space", None),
            P(),
            P("section", None, None, None, None, "space", None),
            P("section", None, None, None, "space", None),
            P("section", None, None, None, None, "space", None),
        ),
        out_specs=P("section", None, None, None, None, "space", None),
        check_vma=False,
    )
```

```python
import jax
import jax.numpy as jnp
from jax import lax
from jax.experimental import pallas as pl
from jax.experimental.pallas import tpu as pltpu
from jax.sharding import PartitionSpec as P


LZ = 16
KINETIC = 1.0 / 6.0
QUARTIC = 1.0 / 216.0
SPIN_WEIGHT = 1.0 / 6.0
SMEAR_WEIGHT = 0.1
AXES = ("section", "space")
VMEM = pltpu.VMEM
PATHS = (
    (
        (1, 0, 0), (0, 0, 0), (0, 1, 0), (1, 1, 0), (1, 2, 0), (0, 2, 0), (0, 3, 0), (1, 3, 0),
        (1, 3, 1), (0, 3, 1), (0, 2, 1), (1, 2, 1), (1, 1, 1), (0, 1, 1), (0, 0, 1), (1, 0, 1),
    ),
    (
        (3, 0, 0), (2, 0, 0), (2, 1, 0), (3, 1, 0), (3, 2, 0), (2, 2, 0), (2, 3, 0), (3, 3, 0),
        (3, 3, 1), (2, 3, 1), (2, 2, 1), (3, 2, 1), (3, 1, 1), (2, 1, 1), (2, 0, 1), (3, 0, 1),
    ),
)
BLOCKS = 16


def place(half, ring, block, core):
    x, y, z = PATHS[ring][block % BLOCKS]
    return (2 * half + core) * 32 + z * 16 + y * 4 + x


def natural(half, turn, pair):
    return (2 * half + turn) * 32 + pair


def every():
    return [
        (half, ring, block, core)
        for half in range(2)
        for ring in range(2)
        for block in range(BLOCKS)
        for core in range(2)
    ]


def across():
    return [
        (place(h, r, m, c), place(h, r, m + 1, 0) if c else place(h, r, m - 1, 1))
        for h, r, m, c in every()
    ]


def sibling():
    return [(place(h, r, m, c), place(h, r, m, 1 - c)) for h, r, m, c in every()]


def onward():
    return [(place(h, r, m, c), place(1 - h, r, m, c)) for h, r, m, c in every()]


def mate():
    return [(natural(h, t, j), natural(h, 1 - t, j)) for h in range(2) for t in range(2) for j in range(32)]


def spread():
    return [(natural(h, r, 2 * m + c), place(h, r, m, c)) for h, r, m, c in every()]


def collect():
    return [(there, here) for here, there in spread()]


def rows_of(shape):
    return lax.broadcasted_iota(jnp.int32, shape, len(shape) - 2)


def lanes_of(shape):
    return lax.broadcasted_iota(jnp.int32, shape, len(shape) - 1)


def roll(value, by, axis):
    return pltpu.roll(value, by, value.ndim + axis)


def swap_planes(value):
    first = rows_of(value.shape) % 2 == 0
    return jnp.where(first, roll(value, 7, -2), roll(value, 1, -2))


def y_forward(value):
    moved = roll(value, 112, -1)
    return jnp.where(lanes_of(value.shape) < 112, moved, roll(moved, 6, -2))


def y_backward(value):
    moved = roll(value, 16, -1)
    return jnp.where(lanes_of(value.shape) >= 16, moved, roll(moved, 2, -2))


def z_forward(value):
    inside = lanes_of(value.shape) % LZ < LZ - 1
    return jnp.where(inside, roll(value, 127, -1), roll(value, LZ - 1, -1))


def z_backward(value):
    inside = lanes_of(value.shape) % LZ > 0
    return jnp.where(inside, roll(value, 1, -1), roll(value, 129 - LZ, -1))


def add(one, other):
    return [a + b for a, b in zip(one, other)]


def scaled(factor, field):
    return [factor * a for a in field]


def link_at(ref, base):
    def entry(row, column):
        return ref[base + 3 * row + column], ref[base + 9 + 3 * row + column]

    return entry


def product(entry, field, dagger, total=None):
    real, imag = [], []
    for out in range(3):
        sum_real = None if total is None else total[out]
        sum_imag = None if total is None else total[3 + out]
        for inner in range(3):
            link_real, link_imag = entry(inner, out) if dagger else entry(out, inner)
            field_real, field_imag = field[inner], field[3 + inner]
            cross_real, cross_imag = link_imag * field_imag, link_imag * field_real
            part_real, part_imag = link_real * field_real, link_real * field_imag
            if dagger:
                part_real, part_imag = part_real + cross_real, part_imag - cross_imag
            else:
                part_real, part_imag = part_real - cross_real, part_imag + cross_imag
            sum_real = part_real if sum_real is None else sum_real + part_real
            sum_imag = part_imag if sum_imag is None else sum_imag + part_imag
        real.append(sum_real)
        imag.append(sum_imag)
    return real + imag


INNER, ALONG_Y, ALONG_Z = 0, 18, 36


def within(links, field):
    total = scaled(-6.0, field)
    total = product(link_at(links, ALONG_Y), [y_forward(a) for a in field], False, total)
    back = product(link_at(links, ALONG_Y), field, True)
    total = add(total, [y_backward(a) for a in back])
    total = product(link_at(links, ALONG_Z), [z_forward(a) for a in field], False, total)
    back = product(link_at(links, ALONG_Z), field, True)
    total = add(total, [z_backward(a) for a in back])
    return product(link_at(links, INNER), [swap_planes(a) for a in field], False, total)


LADDER, LEVEL, TIME = 0, 18, 27


def level_entry(ref):
    def entry(row, column):
        if row == column:
            return ref[LEVEL + row], None
        slot = min(row, column) + max(row, column) - 1
        imag = ref[LEVEL + 6 + slot]
        return ref[LEVEL + 3 + slot], imag if row < column else -imag

    return entry


def hermitian_product(entry, field):
    real, imag = [], []
    for out in range(3):
        sum_real = sum_imag = None
        for inner in range(3):
            link_real, link_imag = entry(out, inner)
            part_real, part_imag = link_real * field[inner], link_real * field[3 + inner]
            if link_imag is not None:
                part_real = part_real - link_imag * field[3 + inner]
                part_imag = part_imag + link_imag * field[inner]
            sum_real = part_real if sum_real is None else sum_real + part_real
            sum_imag = part_imag if sum_imag is None else sum_imag + part_imag
        real.append(sum_real)
        imag.append(sum_imag)
    return real + imag


def spin_term(others, field):
    up, down = [a[0] for a in field], [a[1] for a in field]
    ladder, level = link_at(others, LADDER), level_entry(others)
    upper = add(hermitian_product(level, up), product(ladder, down, False))
    lower = product(ladder, up, True)
    lower = [a - b for a, b in zip(lower, hermitian_product(level, down))]
    return [jnp.stack([a, b]) for a, b in zip(upper, lower)]


def load(ref, column):
    return [ref[pl.ds(column * 12 + 2 * part, 2)] for part in range(6)]


def store(ref, column, field):
    for part in range(6):
        ref[pl.ds(column * 12 + 2 * part, 2)] = field[part]


def prepare(field, links, own_side, partial_ref, across_ref, sibling_ref, column):
    partial = within(links, field)
    turned = [swap_planes(a) for a in partial]
    store(partial_ref, column, partial)
    store(across_ref, column, [jnp.where(own_side, f, t) for f, t in zip(field, turned)])
    store(sibling_ref, column, [jnp.where(own_side, t, f) for f, t in zip(field, turned)])


def two_laplacians(field, partial, from_across, from_sibling, links, outer, own_side):
    beyond = [
        swap_planes(jnp.where(own_side, s, a)) for a, s in zip(from_across, from_sibling)
    ]
    rim = [jnp.where(own_side, a, s) for a, s in zip(from_across, from_sibling)]
    single = product(link_at(outer, 0), beyond, False, partial)
    rim = product(link_at(outer, 0), field, True, rim)
    double = product(link_at(outer, 0), rim, False, within(links, single))
    return single, double


def kernel_call(body, inputs, outputs, pinned=True):
    if pinned:
        inputs = [pltpu.with_memory_space_constraint(value, VMEM) for value in inputs]
    spec = pl.BlockSpec(memory_space=VMEM)
    shapes = [VMEM(shape, jnp.float32) for shape in outputs]
    return pl.pallas_call(
        body,
        in_specs=[spec] * len(inputs),
        out_specs=[spec] * len(outputs),
        out_shape=shapes,
        compiler_params=pltpu.CompilerParams(vmem_limit_bytes=32 * 1024 * 1024),
    )(*inputs)


FIELD = (24, 8, 128)
SIDE, RING, HALF = 0, 1, 2


def own_columns(field, core, message, base):
    for column in range(2):
        for part in range(6):
            for spin in range(2):
                picked = jnp.where(core, field[part, spin, 2 + column], field[part, spin, column])
                message[base + column * 12 + part * 2 + spin] = picked


def pack_magnetic(magnetic, others):
    def raw(axis, imag, row, column):
        return magnetic[axis * 18 + imag * 9 + row * 3 + column]

    def real(axis, row, column):
        return 0.5 * (raw(axis, 0, row, column) + raw(axis, 0, column, row))

    def imag(axis, row, column):
        return 0.5 * (raw(axis, 1, row, column) - raw(axis, 1, column, row))

    for row in range(3):
        for column in range(3):
            at = LADDER + 3 * row + column
            others[at] = real(0, row, column) + imag(1, row, column)
            others[at + 9] = imag(0, row, column) - real(1, row, column)
        others[LEVEL + row] = real(2, row, row)
    for slot, (row, column) in enumerate(((0, 1), (0, 2), (1, 2))):
        others[LEVEL + 3 + slot] = real(2, row, column)
        others[LEVEL + 6 + slot] = imag(2, row, column)


def pack_others(magnetic, time, others):
    pack_magnetic(magnetic, others)
    others[pl.ds(TIME, 18)] = time[...]


def first_message(own_links, mate_links, carried, marks, message):
    core = marks[RING] > 0
    for at in range(54):
        message[at] = jnp.where(core, mate_links[at], own_links[at])
    own_columns(carried, core, message, 54)


def second_message(own_others, mate_others, source, marks, message):
    core = marks[RING] > 0
    for at in range(45):
        message[at] = jnp.where(core, mate_others[at], own_others[at])
    own_columns(source, core, message, 45)


def third_message(own_links, mate_links, own_others, mate_others, marks, message):
    core = marks[RING] > 0
    for at in range(54):
        message[at] = jnp.where(core, own_links[at], mate_links[at])
    for at in range(45):
        message[54 + at] = jnp.where(core, own_others[at], mate_others[at])


def arrange(got, links, plain, edge):
    first = rows_of((8, 128)) % 2 == 0
    links[pl.ds(18, 36)] = got[pl.ds(18, 36)]
    plain[...] = got[pl.ds(0, 18)]
    for row in range(3):
        for column in range(3):
            at, turned = 3 * row + column, 3 * column + row
            links[at] = jnp.where(first, got[at], swap_planes(got[turned]))
            links[at + 9] = jnp.where(first, got[at + 9], -swap_planes(got[turned + 9]))
    for at in range(9):
        edge[at] = jnp.where(first, swap_planes(got[at + 9]), got[at])


def outgoing(from_across, from_sibling, plain, marks, outer):
    first = rows_of((8, 128)) % 2 == 0
    upper_core = jnp.logical_xor(marks[SIDE] > 0, first)
    for row in range(3):
        for column in range(3):
            at, turned = 3 * row + column, 24 + 3 * column + row
            edge = jnp.where(upper_core, from_sibling[turned], from_across[turned])
            outer[at] = jnp.where(first, swap_planes(edge), plain[at])
            outer[at + 9] = jnp.where(first, -edge, plain[at + 9])


def begin(got, marks, field, links, plain, edge, partial, to_across, to_sibling):
    arrange(got, links, plain, edge)
    own_side = marks[SIDE] > 0

    def one_column(column, carry):
        values = [got[pl.ds(54 + column * 12 + part * 2, 2)] for part in range(6)]
        store(field, column, values)
        prepare(values, links, own_side, partial, to_across, to_sibling, column)
        return carry

    lax.fori_loop(0, 2, one_column, 0)
    to_across[pl.ds(24, 9)] = edge[...]
    to_sibling[pl.ds(24, 9)] = edge[...]


def step_a(field, partial, from_across, from_sibling, links, outer, others, own_side):
    single, double = two_laplacians(field, partial, from_across, from_sibling, links, outer, own_side)
    spin = spin_term(others, field)
    return [
        f + (0.5 * KINETIC) * s + (0.5 * QUARTIC) * d + (0.5 * SPIN_WEIGHT) * b
        for f, s, d, b in zip(field, single, double, spin)
    ]


def first_half(field, partial, from_across, from_sibling, links, outer, others, marks, *outs):
    turned_field, *messages = outs
    own_side = marks[SIDE] > 0

    def one_column(column, carry):
        values = step_a(
            load(field, column), load(partial, column), load(from_across, column),
            load(from_sibling, column), links, outer, others, own_side,
        )
        values = product(link_at(others, TIME), values, True)
        store(turned_field, column, values)
        prepare(values, links, own_side, *messages, column)
        return carry

    lax.fori_loop(0, 2, one_column, 0)


def second_half(field, partial, from_across, from_sibling, links, outer, others, source, marks, *rest):
    *after, result = rest[:-3] if len(rest) > 1 else rest
    messages = rest[-3:] if len(rest) > 1 else None
    own_side = marks[SIDE] > 0

    def one_column(column, carry):
        values = step_a(
            load(field, column), load(partial, column), load(from_across, column),
            load(from_sibling, column), links, outer, others, own_side,
        )
        values = add(values, load(source, column))
        store(result, column, values)
        if messages is not None:
            prepare(values, after[0], own_side, *messages, column)
        return carry

    lax.fori_loop(0, 2, one_column, 0)
    if len(after) > 1:
        for message in messages[1:]:
            message[pl.ds(24, 9)] = after[1][...]


def only_prepare(field, links, marks, *messages):
    own_side = marks[SIDE] > 0

    def one_column(column, carry):
        prepare(load(field, column), links, own_side, *messages, column)
        return carry

    lax.fori_loop(0, 2, one_column, 0)


def smear_start(early_a, early_b, late_a, late_b, links_a, links_b, marks, field_a, field_b, *messages):
    own_side = marks[SIDE] > 0
    half = marks[HALF] > 0
    for turn, early, late, links, field in (
        (0, early_a, late_a, links_a, field_a),
        (1, early_b, late_b, links_b, field_b),
    ):

        def one_column(column, carry):
            values = [jnp.where(half, b, a) for a, b in zip(load(early, column), load(late, column))]
            store(field, column, values)
            prepare(values, links, own_side, *[ref.at[pl.ds(24 * turn, 24)] for ref in messages], column)
            return carry

        lax.fori_loop(0, 2, one_column, 0)


def smear_end(field_a, field_b, partial, from_across, from_sibling, links_a, links_b, outer_a, outer_b, marks, out):
    own_side = marks[SIDE] > 0
    for turn, field_ref, links, outer in ((0, field_a, links_a, outer_a), (1, field_b, links_b, outer_b)):

        def one_column(column, carry):
            at = column + 2 * turn
            field = load(field_ref, column)
            single, double = two_laplacians(
                field, load(partial, at), load(from_across, at), load(from_sibling, at),
                links, outer, own_side,
            )
            values = [
                f + (2 * SMEAR_WEIGHT) * s + (SMEAR_WEIGHT * SMEAR_WEIGHT) * d
                for f, s, d in zip(field, single, double)
            ]
            store(out, at, values)
            return carry

        lax.fori_loop(0, 2, one_column, 0)


def for_mate(got, marks, message):
    core = marks[RING] > 0
    for at in range(24):
        message[at] = jnp.where(core, got[at], got[24 + at])


def deliver(got, other, marks, out):
    core = marks[RING] > 0
    for column in range(2):
        for part in range(6):
            for spin in range(2):
                at = column * 12 + part * 2 + spin
                mine = jnp.where(core, got[24 + at], got[at])
                out[part, spin, column] = jnp.where(core, other[at], mine)
                out[part, spin, 2 + column] = jnp.where(core, mine, other[at])


def registers(value, lead):
    rows = value.reshape(lead + (2, 4, 128))
    return jnp.swapaxes(rows, -3, -2).reshape(lead + (8, 128))


def exchange(to_across, to_sibling):
    return lax.ppermute(to_across, AXES, across()), lax.ppermute(to_sibling, AXES, sibling())


def full(flag):
    return jnp.broadcast_to(flag.astype(jnp.float32), (8, 128))


def local(carried, source_field, source_slice, space_links, time_links, magnetic):
    section, space = lax.axis_index("section"), lax.axis_index("space")
    core, half, ring = section % 2, section // 2, space % 4 // 2
    first = (jnp.arange(8) % 2)[:, None] == core
    side = jnp.broadcast_to(first.astype(jnp.float32), (8, 128))
    marks = jnp.stack([side, full(core == 1), full(half == 1)])

    carried = registers(carried, (6, 2, 4))
    source_field = registers(source_field, (6, 2, 4))
    space_links = registers(space_links, (54,))
    time_links = registers(time_links, (18,))
    magnetic = registers(magnetic, (54,))

    mate_links = lax.ppermute(space_links, AXES, mate())
    (own_others,) = kernel_call(pack_others, [magnetic, time_links], [(45, 8, 128)], False)
    mate_others = lax.ppermute(own_others, AXES, mate())
    (message,) = kernel_call(first_message, [space_links, mate_links, carried, marks], [(78, 8, 128)], False)
    got = lax.ppermute(message, AXES, spread())
    (message,) = kernel_call(
        second_message, [own_others, mate_others, source_field, marks], [(69, 8, 128)], False
    )
    others_a = lax.ppermute(message, AXES, spread())
    (message,) = kernel_call(
        third_message, [space_links, mate_links, own_others, mate_others, marks], [(99, 8, 128)], False
    )
    got_b = lax.ppermute(message, AXES, spread())

    with_edge = (33, 8, 128)
    field, links_a, plain_a, _, partial, to_across, to_sibling = kernel_call(
        begin,
        [got, marks],
        [FIELD, (54, 8, 128), (18, 8, 128), (9, 8, 128), FIELD, with_edge, with_edge],
    )
    from_across, from_sibling = exchange(to_across, to_sibling)
    (outer_a,) = kernel_call(outgoing, [from_across, from_sibling, plain_a, marks], [(18, 8, 128)])
    links_b, plain_b, edge_b = kernel_call(
        arrange, [got_b], [(54, 8, 128), (18, 8, 128), (9, 8, 128)]
    )
    others_b = got_b[54:]
    source = others_a[45:]
    here = lax.dynamic_slice_in_dim(source_slice, 2 * ring, 2)
    sources = [
        jnp.repeat((here == 2 * half + turn).astype(jnp.float32), 12).reshape(24, 1, 1) * source
        for turn in range(2)
    ]
    links, others = (links_a, links_b), (others_a, others_b)
    outer_b = None
    results = []
    for phase in range(2):
        for turn in range(2):
            if phase == 0 and turn == 1:
                (outer_b,) = kernel_call(
                    outgoing, [from_across, from_sibling, plain_b, marks], [(18, 8, 128)]
                )
            outer = (outer_a, outer_b)[turn]
            field, partial, to_across, to_sibling = kernel_call(
                first_half,
                [field, partial, from_across, from_sibling, links[turn], outer, others[turn], marks],
                [FIELD] * 4,
            )
            from_across, from_sibling = exchange(to_across, to_sibling)
            inputs = [field, partial, from_across, from_sibling, links[turn], outer, others[turn]]
            inputs += [sources[turn], marks]
            if turn == 0:
                more, size = ([edge_b], with_edge) if phase == 0 else ([], FIELD)
                field, partial, to_across, to_sibling = kernel_call(
                    second_half, inputs + [links_b] + more, [FIELD, FIELD, size, size]
                )
                from_across, from_sibling = exchange(to_across, to_sibling)
            else:
                (field,) = kernel_call(second_half, inputs, [FIELD])
            results.append(field)
        if phase == 0:
            field = lax.ppermute(field, AXES, onward())
            partial, to_across, to_sibling = kernel_call(
                only_prepare, [field, links_a, marks], [FIELD] * 3
            )
            from_across, from_sibling = exchange(to_across, to_sibling)

    both = (48, 8, 128)
    field_a, field_b, partial, to_across, to_sibling = kernel_call(
        smear_start, results + [links_a, links_b, marks], [FIELD, FIELD, both, both, both]
    )
    from_across, from_sibling = exchange(to_across, to_sibling)
    (out,) = kernel_call(
        smear_end,
        [field_a, field_b, partial, from_across, from_sibling, links_a, links_b, outer_a, outer_b, marks],
        [both],
    )
    got = lax.ppermute(out, AXES, collect())
    (message,) = kernel_call(for_mate, [got, marks], [FIELD])
    other = lax.ppermute(message, AXES, mate())
    (out,) = kernel_call(deliver, [got, other, marks], [(6, 2, 4, 8, 128)])
    out = jnp.swapaxes(out.reshape(2, 3, 2, 4, 4, 2, 128), -3, -2)
    return out.reshape(1, 2, 3, 2, 4, 2, 512)


def solution(mesh):
    return jax.shard_map(
        local,
        mesh=mesh,
        in_specs=(
            P(None, None, None, None, "space", None),
            P(None, None, None, None, "space", None),
            P(),
            P("section", None, None, None, None, "space", None),
            P("section", None, None, None, "space", None),
            P("section", None, None, None, None, "space", None),
        ),
        out_specs=P("section", None, None, None, None, "space", None),
        check_vma=False,
    )
```

```python
import functools

import jax
import jax.numpy as jnp
from jax import lax
from jax.experimental import pallas as pl
from jax.experimental.pallas import tpu as pltpu
from jax.sharding import PartitionSpec as P


LZ = 16
KINETIC = 1.0 / 6.0
QUARTIC = 1.0 / 216.0
SPIN_WEIGHT = 1.0 / 6.0
SMEAR_WEIGHT = 0.1
AXES = ("section", "space")
VMEM = pltpu.VMEM
PAIRS = 32
SLICES = 4


def chip(pair):
    at = min(pair, PAIRS - 1 - pair)
    y, x = divmod(at, 4)
    return (x if y % 2 == 0 else 3 - x), y, pair // 16


def place(half, core, pair):
    x, y, z = chip(pair % PAIRS)
    return (2 * half + core) * 32 + z * 16 + y * 4 + x


def natural(half, core, pair):
    return (2 * half + core) * 32 + pair


EVERY = [(half, core, pair) for half in range(2) for core in range(2) for pair in range(PAIRS)]
SPREAD = [(natural(h, c, j), place(h, c, j)) for h, c, j in EVERY]
COLLECT = [[(place(h, c, j), natural(h ^ way, c, j)) for h, c, j in EVERY] for way in range(2)]
UP = [(place(h, c, j), place(h, 1 - c, j + 1)) for h, c, j in EVERY]
DOWN = [(place(h, c, j), place(h, 1 - c, j - 1)) for h, c, j in EVERY]
SIBLING = [(place(h, c, j), place(h, 1 - c, j)) for h, c, j in EVERY]
FACING = [(place(h, c, j), place(1 - h, c, j)) for h, c, j in EVERY]


def rows_of(shape):
    return lax.broadcasted_iota(jnp.int32, shape, len(shape) - 2)


def lanes_of(shape):
    return lax.broadcasted_iota(jnp.int32, shape, len(shape) - 1)


def roll(value, by, axis):
    return pltpu.roll(value, by, value.ndim + axis)


def swap_planes(value):
    first = rows_of(value.shape) % 2 == 0
    return jnp.where(first, roll(value, 7, -2), roll(value, 1, -2))


def y_forward(value):
    moved = roll(value, 112, -1)
    return jnp.where(lanes_of(value.shape) < 112, moved, roll(moved, 6, -2))


def y_backward(value):
    moved = roll(value, 16, -1)
    return jnp.where(lanes_of(value.shape) >= 16, moved, roll(moved, 2, -2))


def z_forward(value):
    inside = lanes_of(value.shape) % LZ < LZ - 1
    return jnp.where(inside, roll(value, 127, -1), roll(value, LZ - 1, -1))


def z_backward(value):
    inside = lanes_of(value.shape) % LZ > 0
    return jnp.where(inside, roll(value, 1, -1), roll(value, 129 - LZ, -1))


def add(one, other):
    return [a + b for a, b in zip(one, other)]


def scaled(factor, field):
    return [factor * a for a in field]


def link_at(ref, base):
    def entry(row, column):
        return ref[base + 3 * row + column], ref[base + 9 + 3 * row + column]

    return entry


def product(entry, field, dagger, total=None):
    real, imag = [], []
    for out in range(3):
        sum_real = None if total is None else total[out]
        sum_imag = None if total is None else total[3 + out]
        for inner in range(3):
            link_real, link_imag = entry(inner, out) if dagger else entry(out, inner)
            field_real, field_imag = field[inner], field[3 + inner]
            cross_real, cross_imag = link_imag * field_imag, link_imag * field_real
            part_real, part_imag = link_real * field_real, link_real * field_imag
            if dagger:
                part_real, part_imag = part_real + cross_real, part_imag - cross_imag
            else:
                part_real, part_imag = part_real - cross_real, part_imag + cross_imag
            sum_real = part_real if sum_real is None else sum_real + part_real
            sum_imag = part_imag if sum_imag is None else sum_imag + part_imag
        real.append(sum_real)
        imag.append(sum_imag)
    return real + imag


ALONG_X, ALONG_Y, ALONG_Z = 0, 18, 36


def within(links, inner, field):
    total = scaled(-6.0, field)
    total = product(link_at(links, ALONG_Y), [y_forward(a) for a in field], False, total)
    back = product(link_at(links, ALONG_Y), field, True)
    total = add(total, [y_backward(a) for a in back])
    total = product(link_at(links, ALONG_Z), [z_forward(a) for a in field], False, total)
    back = product(link_at(links, ALONG_Z), field, True)
    total = add(total, [z_backward(a) for a in back])
    return product(link_at(inner, 0), [swap_planes(a) for a in field], False, total)


LADDER, LEVEL, TIME = 0, 18, 27


def level_entry(ref):
    def entry(row, column):
        if row == column:
            return ref[LEVEL + row], None
        slot = min(row, column) + max(row, column) - 1
        imag = ref[LEVEL + 6 + slot]
        return ref[LEVEL + 3 + slot], imag if row < column else -imag

    return entry


def hermitian_product(entry, field):
    real, imag = [], []
    for out in range(3):
        sum_real = sum_imag = None
        for inner in range(3):
            link_real, link_imag = entry(out, inner)
            part_real, part_imag = link_real * field[inner], link_real * field[3 + inner]
            if link_imag is not None:
                part_real = part_real - link_imag * field[3 + inner]
                part_imag = part_imag + link_imag * field[inner]
            sum_real = part_real if sum_real is None else sum_real + part_real
            sum_imag = part_imag if sum_imag is None else sum_imag + part_imag
        real.append(sum_real)
        imag.append(sum_imag)
    return real + imag


def spin_term(others, field):
    up, down = [a[0] for a in field], [a[1] for a in field]
    ladder, level = link_at(others, LADDER), level_entry(others)
    upper = add(hermitian_product(level, up), product(ladder, down, False))
    lower = product(ladder, up, True)
    lower = [a - b for a, b in zip(lower, hermitian_product(level, down))]
    return [jnp.stack([a, b]) for a, b in zip(upper, lower)]


def load(ref, column):
    return [ref[pl.ds(column * 12 + 2 * part, 2)] for part in range(6)]


def store(ref, column, field):
    for part in range(6):
        ref[pl.ds(column * 12 + 2 * part, 2)] = field[part]


def prepare(field, links, inner, lower, partial_ref, below_ref, above_ref, column):
    partial = within(links, inner, field)
    turned = [swap_planes(a) for a in partial]
    store(partial_ref, column, partial)
    store(below_ref, column, [jnp.where(lower, f, t) for f, t in zip(field, turned)])
    store(above_ref, column, [jnp.where(lower, t, f) for f, t in zip(field, turned)])


def two_laplacians(field, partial, from_below, from_above, links, inner, outer, lower):
    beyond = [
        swap_planes(jnp.where(lower, s, a)) for a, s in zip(from_below, from_above)
    ]
    rim = [jnp.where(lower, a, s) for a, s in zip(from_below, from_above)]
    single = product(link_at(outer, 0), beyond, False, partial)
    rim = product(link_at(outer, 0), field, True, rim)
    double = product(link_at(outer, 0), rim, False, within(links, inner, single))
    return single, double


def kernel_call(body, inputs, outputs, far=(), near=(), scratch=()):
    spec = pl.BlockSpec(memory_space=VMEM)
    spaces = [pltpu.HBM if at in far else pltpu.SMEM if at in near else VMEM for at in range(len(inputs))]
    inputs = [
        value if at in near else pltpu.with_memory_space_constraint(value, space)
        for at, (value, space) in enumerate(zip(inputs, spaces))
    ]
    shapes = [VMEM(shape, jnp.float32) for shape in outputs]
    return pl.pallas_call(
        body,
        in_specs=[pl.BlockSpec(memory_space=space) for space in spaces],
        out_specs=[spec] * len(outputs),
        out_shape=shapes,
        scratch_shapes=list(scratch),
        compiler_params=pltpu.CompilerParams(vmem_limit_bytes=32 * 1024 * 1024),
    )(*inputs)


FIELD = (12, 8, 128)
WITH_EDGE = (21, 8, 128)
WITH_RIM = (18, 8, 128)
CORE, HALF, TWIST = 0, 1, 2


def own_column(field, marks, message, base):
    half, twist = marks[HALF] > 0, marks[TWIST] > 0
    for part in range(6):
        for spin in range(2):
            low = jnp.where(twist, field[part, spin, 1], field[part, spin, 0])
            high = jnp.where(twist, field[part, spin, 3], field[part, spin, 2])
            message[base + part * 2 + spin] = jnp.where(half, high, low)


def pack_magnetic(magnetic, others):
    def raw(axis, imag, row, column):
        return magnetic[axis * 18 + imag * 9 + row * 3 + column]

    def real(axis, row, column):
        return 0.5 * (raw(axis, 0, row, column) + raw(axis, 0, column, row))

    def imag(axis, row, column):
        return 0.5 * (raw(axis, 1, row, column) - raw(axis, 1, column, row))

    for row in range(3):
        for column in range(3):
            at = LADDER + 3 * row + column
            others[at] = real(0, row, column) + imag(1, row, column)
            others[at + 9] = imag(0, row, column) - real(1, row, column)
        others[LEVEL + row] = real(2, row, row)
    for slot, (row, column) in enumerate(((0, 1), (0, 2), (1, 2))):
        others[LEVEL + 3 + slot] = real(2, row, column)
        others[LEVEL + 6 + slot] = imag(2, row, column)


def pack(space, time, magnetic, carried, own, field, raw, sems):
    copies = [
        pltpu.make_async_copy(source, target, sems.at[at])
        for at, (source, target) in enumerate(
            ((magnetic, raw), (space, own.at[pl.ds(0, 54)]), (time, own.at[pl.ds(54 + TIME, 18)]), (carried, field))
        )
    ]
    for copy in copies:
        copy.start()
    copies[0].wait()
    pack_magnetic(raw, own.at[pl.ds(54, 27)])
    for copy in copies[1:]:
        copy.wait()


def first_message(own, carried, marks, message):
    message[pl.ds(0, 54)] = own[pl.ds(0, 54)]
    own_column(carried, marks, message, 54)


def second_message(own, source, marks, message):
    message[pl.ds(0, 45)] = own[pl.ds(54, 45)]
    own_column(source, marks, message, 45)


def third_message(size, own, facing, message):
    message[pl.ds(0, size)] = own[pl.ds(0, size)]
    message[pl.ds(size, size)] = facing[...]


def pick(timeslice, own, facing, beside, marks, size, out):
    same_half = (marks[HALF] > 0) == (timeslice // 2 == 1)
    same_core = (marks[CORE] > 0) == (timeslice % 2 == 1)
    for at in range(size):
        mine = jnp.where(same_half, own[at], facing[at])
        theirs = jnp.where(same_half, beside[at], beside[size + at])
        out[at] = jnp.where(same_core, mine, theirs)


def arrange(links, inner, edge):
    first = rows_of((8, 128)) % 2 == 0
    turned = [swap_planes(links[at]) for at in range(18)]
    for row in range(3):
        for column in range(3):
            at, across = 3 * row + column, 3 * column + row
            inner[at] = jnp.where(first, links[at], turned[across])
            inner[at + 9] = jnp.where(first, links[at + 9], -turned[across + 9])
    for at in range(9):
        edge[at] = jnp.where(first, turned[at + 9], links[at])


def outgoing(from_below, links, outer):
    first = rows_of((8, 128)) % 2 == 0
    for row in range(3):
        for column in range(3):
            at, turned = 3 * row + column, 12 + 3 * column + row
            edge = from_below[turned]
            outer[at] = jnp.where(first, swap_planes(edge), links[at])
            outer[at + 9] = jnp.where(first, -edge, links[at + 9])


def begin(own, facing, beside, marks, field, links, inner, partial, to_below, to_above):
    pick(0, own, facing, beside, marks, 54, links)
    arrange(links, inner, to_above.at[pl.ds(12, 9)])
    lower = rows_of((8, 128)) % 2 == 0
    values = [own[pl.ds(54 + part * 2, 2)] for part in range(6)]
    store(field, 0, values)
    prepare(values, links, inner, lower, partial, to_below, to_above, 0)


def later_links(own, facing, beside, marks, *outs):
    for timeslice in range(1, SLICES):
        links, inner, edge = outs[3 * timeslice - 3 : 3 * timeslice]
        pick(timeslice, own, facing, beside, marks, 54, links)
        arrange(links, inner, edge)


def other_links(first, own, facing, beside, marks, *outs):
    for at, others in enumerate(outs):
        pick(first + at, own, facing, beside, marks, 45, others)


def step_a(field, partial, from_below, from_above, links, inner, outer, others, lower):
    single, double = two_laplacians(field, partial, from_below, from_above, links, inner, outer, lower)
    spin = spin_term(others, field)
    return [
        f + (0.5 * KINETIC) * s + (0.5 * QUARTIC) * d + (0.5 * SPIN_WEIGHT) * b
        for f, s, d, b in zip(field, single, double, spin)
    ]


def masked_sources(source_slice, others, marks, _, *outs):
    half, twist = marks[HALF] > 0, marks[TWIST] > 0
    for timeslice, out in enumerate(outs):
        on = [jnp.where(source_slice[column] == timeslice, 1.0, 0.0) for column in range(4)]
        weight = jnp.where(half, jnp.where(twist, on[3], on[2]), jnp.where(twist, on[1], on[0]))
        for at in range(12):
            out[at] = weight * others[45 + at]


def first_half(field, partial, from_below, from_above, links, inner, outer, others, *rest):
    rims, (turned_field, *messages) = rest[:-4], rest[-4:]
    lower = rows_of((8, 128)) % 2 == 0
    values = step_a(
        load(field, 0), load(partial, 0), load(from_below, 0), load(from_above, 0),
        links, inner, outer, others, lower,
    )
    values = product(link_at(others, TIME), values, True)
    store(turned_field, 0, values)
    prepare(values, links, inner, lower, *messages, 0)
    for rim, message in zip(rims, messages[1:]):
        message[pl.ds(12, 6)] = rim[...]


def second_half(field, partial, from_below, from_above, links, inner, outer, others, source, *rest):
    lower = rows_of((8, 128)) % 2 == 0
    values = step_a(
        load(field, 0), load(partial, 0), load(from_below, 0), load(from_above, 0),
        links, inner, outer, others, lower,
    )
    values = add(values, load(source, 0))
    if len(rest) == 4:
        result, *messages = rest
        store(result, 0, values)
        prepare(values, links, inner, lower, *messages, 0)
        return
    next_links, next_inner, next_edge, result, *messages = rest
    store(result, 0, values)
    prepare(values, next_links, next_inner, lower, *messages, 0)
    messages[2][pl.ds(12, 9)] = next_edge[...]


def smear_start(field, links, inner, partial_ref, rim_below, rim_above):
    first = rows_of((8, 128)) % 2 == 0
    partial = within(links, inner, load(field, 0))
    store(partial_ref, 0, partial)
    for part in range(6):
        up, down = partial[part][0], partial[part][1]
        rim_below[part] = jnp.where(first, up, swap_planes(down))
        rim_above[part] = jnp.where(first, swap_planes(up), down)


def smeared(field, partial, beyond, rim, links, inner, outer):
    single = product(link_at(outer, 0), beyond, False, partial)
    rim = product(link_at(outer, 0), field, True, rim)
    double = product(link_at(outer, 0), rim, False, within(links, inner, single))
    return [
        f + (2 * SMEAR_WEIGHT) * s + (SMEAR_WEIGHT * SMEAR_WEIGHT) * d
        for f, s, d in zip(field, single, double)
    ]


def smear_end(field, partial, from_below, from_above, rims_below, rims_above, links, inner, outer, out):
    lower = rows_of((8, 128)) % 2 == 0
    beyond = [
        swap_planes(jnp.where(lower, a, b)) for a, b in zip(load(from_above, 0), load(from_below, 0))
    ]
    rim = []
    for part in range(6):
        below, above = rims_below[12 + part], rims_above[12 + part]
        up = jnp.where(lower, below, swap_planes(above))
        down = jnp.where(lower, swap_planes(below), above)
        rim.append(jnp.stack([up, down]))
    store(out, 0, smeared(load(field, 0), load(partial, 0), beyond, rim, links, inner, outer))


def last_smear_end(field, partial, from_below, from_above, links, inner, outer, done_0, done_1, done_2, marks, mine, theirs):
    lower = rows_of((8, 128)) % 2 == 0
    core = marks[CORE] > 0
    below, above = load(from_below, 0), load(from_above, 0)
    beyond = [swap_planes(jnp.where(lower, a, b)) for a, b in zip(above, below)]
    rim = [jnp.where(lower, b, a) for a, b in zip(above, below)]
    last = smeared(load(field, 0), load(partial, 0), beyond, rim, links, inner, outer)
    for level, pair in enumerate(((load(done_0, 0), load(done_1, 0)), (load(done_2, 0), last))):
        store(mine, level, [jnp.where(core, b, a) for a, b in zip(*pair)])
        store(theirs, level, [jnp.where(core, a, b) for a, b in zip(*pair)])


def both_columns(way, mine, other, marks, *rest):
    half, twist = (marks[HALF] > 0) == (way == 0), marks[TWIST] > 0
    out = rest[-1]
    for at in range(12):
        own, beside = jnp.where(half, mine[12 + at], mine[at]), jnp.where(half, other[12 + at], other[at])
        out[at] = jnp.where(twist, beside, own)
        out[12 + at] = jnp.where(twist, own, beside)


def deliver(got0, got1, marks, out):
    half = marks[HALF] > 0
    for column in range(2):
        for part in range(6):
            for spin in range(2):
                at = column * 12 + part * 2 + spin
                out[part, spin, column] = jnp.where(half, got1[at], got0[at])
                out[part, spin, 2 + column] = jnp.where(half, got0[at], got1[at])


def registers(value, lead):
    rows = value.reshape(lead + (2, 4, 128))
    return jnp.swapaxes(rows, -3, -2).reshape(lead + (8, 128))


def exchange(to_below, to_above):
    return lax.ppermute(to_above, AXES, UP), lax.ppermute(to_below, AXES, DOWN)


def full(flag):
    return jnp.broadcast_to(flag.astype(jnp.float32), (8, 128))


def local(carried, source_field, source_slice, space_links, time_links, magnetic):
    section, space = lax.axis_index("section"), lax.axis_index("space")
    core, half = section % 2, section // 2
    x, y, z = space % 4, space // 4 % 4, space // 16
    twist_there = (core + x) % 2
    twist = (core + x + y + z) % 2
    marks_there = jnp.stack([full(core == 1), full(half == 1), full(twist_there == 1)])
    marks = jnp.stack([full(core == 1), full(half == 1), full(twist == 1)])

    carried = registers(carried, (6, 2, 4))
    source_field = registers(source_field, (6, 2, 4))
    space_links = registers(space_links, (54,))
    time_links = registers(time_links, (18,))
    magnetic = registers(magnetic, (54,))

    own, carried = kernel_call(
        pack,
        [space_links, time_links, magnetic, carried],
        [(99, 8, 128), (6, 2, 4, 8, 128)],
        far=range(4),
        scratch=[VMEM((54, 8, 128), jnp.float32), pltpu.SemaphoreType.DMA((4,))],
    )
    (message,) = kernel_call(first_message, [own, carried, marks_there], [(66, 8, 128)])
    links_own = lax.ppermute(message, AXES, SPREAD)
    (message,) = kernel_call(second_message, [own, source_field, marks_there], [(57, 8, 128)])
    others_own = lax.ppermute(message, AXES, SPREAD)
    links_facing = lax.ppermute(links_own[:54], AXES, FACING)
    others_facing = lax.ppermute(others_own[:45], AXES, FACING)
    (message,) = kernel_call(
        functools.partial(third_message, 54), [links_own, links_facing], [(108, 8, 128)]
    )
    links_beside = lax.ppermute(message, AXES, SIBLING)
    (message,) = kernel_call(
        functools.partial(third_message, 45), [others_own, others_facing], [(90, 8, 128)]
    )
    others_beside = lax.ppermute(message, AXES, SIBLING)

    field, links_0, inner_0, partial, to_below, to_above = kernel_call(
        begin,
        [links_own, links_facing, links_beside, marks],
        [FIELD, (54, 8, 128), (18, 8, 128), FIELD, FIELD, WITH_EDGE],
    )
    from_below, from_above = exchange(to_below, to_above)
    later = kernel_call(
        later_links,
        [links_own, links_facing, links_beside, marks],
        [(54, 8, 128), (18, 8, 128), (9, 8, 128)] * 3,
    )
    links, inner, edge = [links_0, *later[0::3]], [inner_0, *later[1::3]], [None, *later[2::3]]
    picked = [others_own, others_facing, others_beside, marks]
    others = kernel_call(functools.partial(other_links, 0), picked, [(45, 8, 128)])
    others += kernel_call(functools.partial(other_links, 1), picked, [(45, 8, 128)] * 3)

    sources = kernel_call(
        masked_sources, [source_slice, others_own, marks, to_below], [FIELD] * SLICES, near=(0,)
    )
    outer, done, rims = [], [], []
    for timeslice in range(SLICES):
        outer += kernel_call(outgoing, [from_below, links[timeslice]], [(18, 8, 128)])
        around = [links[timeslice], inner[timeslice], outer[timeslice], others[timeslice]]
        size = WITH_RIM if rims else FIELD
        before = [from_below, from_above]
        field, partial, to_below, to_above = kernel_call(
            first_half, [field, partial, *before, *around, *rims], [FIELD, FIELD, size, size]
        )
        from_below, from_above = exchange(to_below, to_above)
        if rims:
            at = timeslice - 1
            done += kernel_call(
                smear_end,
                [result, smear_partial, *before, from_below, from_above, links[at], inner[at], outer[at]],
                [FIELD],
            )
        inputs = [field, partial, from_below, from_above] + around + [sources[timeslice]]
        if timeslice + 1 < SLICES:
            after = [links[timeslice + 1], inner[timeslice + 1], edge[timeslice + 1]]
            field, partial, to_below, to_above = kernel_call(
                second_half, inputs + after, [FIELD, FIELD, FIELD, WITH_EDGE]
            )
            result = field
            smear_partial, *rims = kernel_call(
                smear_start, [field, links[timeslice], inner[timeslice]], [FIELD] + [(6, 8, 128)] * 2
            )
        else:
            field, partial, to_below, to_above = kernel_call(second_half, inputs, [FIELD] * 4)
        from_below, from_above = exchange(to_below, to_above)

    around = [links[-1], inner[-1], outer[-1]]
    mine, theirs = kernel_call(
        last_smear_end, [field, partial, from_below, from_above, *around, *done, marks], [(24, 8, 128)] * 2
    )
    other = lax.ppermute(theirs, AXES, SIBLING)
    (out1,) = kernel_call(functools.partial(both_columns, 1), [mine, other, marks], [(24, 8, 128)])
    got1 = lax.ppermute(out1, AXES, COLLECT[1])
    (out0,) = kernel_call(functools.partial(both_columns, 0), [mine, other, marks, out1], [(24, 8, 128)])
    got0 = lax.ppermute(out0, AXES, COLLECT[0])
    (out,) = kernel_call(deliver, [got0, got1, marks], [(6, 2, 4, 8, 128)])
    out = jnp.swapaxes(out.reshape(2, 3, 2, 4, 4, 2, 128), -3, -2)
    return out.reshape(1, 2, 3, 2, 4, 2, 512)


def solution(mesh):
    return jax.shard_map(
        local,
        mesh=mesh,
        in_specs=(
            P(None, None, None, None, "space", None),
            P(None, None, None, None, "space", None),
            P(),
            P("section", None, None, None, None, "space", None),
            P("section", None, None, None, "space", None),
            P("section", None, None, None, None, "space", None),
        ),
        out_specs=P("section", None, None, None, None, "space", None),
        check_vma=False,
    )
```

```python
import functools

import jax
import jax.numpy as jnp
from jax import lax
from jax.experimental import pallas as pl
from jax.experimental.pallas import tpu as pltpu
from jax.sharding import PartitionSpec as P


LZ = 16
KINETIC = 1.0 / 6.0
QUARTIC = 1.0 / 216.0
SPIN_WEIGHT = 1.0 / 6.0
SMEAR_WEIGHT = 0.1
AXES = ("section", "space")
VMEM = pltpu.VMEM
PAIRS = 32
SLICES = 4


def chip(pair):
    at = min(pair, PAIRS - 1 - pair)
    y, x = divmod(at, 4)
    return (x if y % 2 == 0 else 3 - x), y, pair // 16


def place(half, core, pair):
    x, y, z = chip(pair % PAIRS)
    return (2 * half + core) * 32 + z * 16 + y * 4 + x


def natural(half, core, pair):
    return (2 * half + core) * 32 + pair


EVERY = [(half, core, pair) for half in range(2) for core in range(2) for pair in range(PAIRS)]
SPREAD = [(natural(h, c, j), place(h, c, j)) for h, c, j in EVERY]
COLLECT = [[(place(h, c, j), natural(h ^ way, c, j)) for h, c, j in EVERY] for way in range(2)]
UP = [(place(h, c, j), place(h, 1 - c, j + 1)) for h, c, j in EVERY]
DOWN = [(place(h, c, j), place(h, 1 - c, j - 1)) for h, c, j in EVERY]
SIBLING = [(place(h, c, j), place(h, 1 - c, j)) for h, c, j in EVERY]
FACING = [(place(h, c, j), place(1 - h, c, j)) for h, c, j in EVERY]


def rows_of(shape):
    return lax.broadcasted_iota(jnp.int32, shape, len(shape) - 2)


def lanes_of(shape):
    return lax.broadcasted_iota(jnp.int32, shape, len(shape) - 1)


def roll(value, by, axis):
    return pltpu.roll(value, by, value.ndim + axis)


def swap_planes(value):
    first = rows_of(value.shape) % 2 == 0
    return jnp.where(first, roll(value, 7, -2), roll(value, 1, -2))


def y_forward(value):
    moved = roll(value, 112, -1)
    return jnp.where(lanes_of(value.shape) < 112, moved, roll(moved, 6, -2))


def y_backward(value):
    moved = roll(value, 16, -1)
    return jnp.where(lanes_of(value.shape) >= 16, moved, roll(moved, 2, -2))


def z_forward(value):
    inside = lanes_of(value.shape) % LZ < LZ - 1
    return jnp.where(inside, roll(value, 127, -1), roll(value, LZ - 1, -1))


def z_backward(value):
    inside = lanes_of(value.shape) % LZ > 0
    return jnp.where(inside, roll(value, 1, -1), roll(value, 129 - LZ, -1))


def add(one, other):
    return [a + b for a, b in zip(one, other)]


def scaled(factor, field):
    return [factor * a for a in field]


def link_at(ref, base):
    def entry(row, column):
        return ref[base + 3 * row + column], ref[base + 9 + 3 * row + column]

    return entry


def product(entry, field, dagger, total=None):
    real, imag = [], []
    for out in range(3):
        sum_real = None if total is None else total[out]
        sum_imag = None if total is None else total[3 + out]
        for inner in range(3):
            link_real, link_imag = entry(inner, out) if dagger else entry(out, inner)
            field_real, field_imag = field[inner], field[3 + inner]
            cross_real, cross_imag = link_imag * field_imag, link_imag * field_real
            part_real, part_imag = link_real * field_real, link_real * field_imag
            if dagger:
                part_real, part_imag = part_real + cross_real, part_imag - cross_imag
            else:
                part_real, part_imag = part_real - cross_real, part_imag + cross_imag
            sum_real = part_real if sum_real is None else sum_real + part_real
            sum_imag = part_imag if sum_imag is None else sum_imag + part_imag
        real.append(sum_real)
        imag.append(sum_imag)
    return real + imag


ALONG_X, ALONG_Y, ALONG_Z = 0, 18, 36


def within(links, inner, field):
    total = scaled(-6.0, field)
    total = product(link_at(links, ALONG_Y), [y_forward(a) for a in field], False, total)
    back = product(link_at(links, ALONG_Y), field, True)
    total = add(total, [y_backward(a) for a in back])
    total = product(link_at(links, ALONG_Z), [z_forward(a) for a in field], False, total)
    back = product(link_at(links, ALONG_Z), field, True)
    total = add(total, [z_backward(a) for a in back])
    return product(link_at(inner, 0), [swap_planes(a) for a in field], False, total)


LADDER, LEVEL, TIME = 0, 18, 27


def level_entry(ref):
    def entry(row, column):
        if row == column:
            return ref[LEVEL + row], None
        slot = min(row, column) + max(row, column) - 1
        imag = ref[LEVEL + 6 + slot]
        return ref[LEVEL + 3 + slot], imag if row < column else -imag

    return entry


def hermitian_product(entry, field):
    real, imag = [], []
    for out in range(3):
        sum_real = sum_imag = None
        for inner in range(3):
            link_real, link_imag = entry(out, inner)
            part_real, part_imag = link_real * field[inner], link_real * field[3 + inner]
            if link_imag is not None:
                part_real = part_real - link_imag * field[3 + inner]
                part_imag = part_imag + link_imag * field[inner]
            sum_real = part_real if sum_real is None else sum_real + part_real
            sum_imag = part_imag if sum_imag is None else sum_imag + part_imag
        real.append(sum_real)
        imag.append(sum_imag)
    return real + imag


def spin_term(others, field):
    up, down = [a[0] for a in field], [a[1] for a in field]
    ladder, level = link_at(others, LADDER), level_entry(others)
    upper = add(hermitian_product(level, up), product(ladder, down, False))
    lower = product(ladder, up, True)
    lower = [a - b for a, b in zip(lower, hermitian_product(level, down))]
    return [jnp.stack([a, b]) for a, b in zip(upper, lower)]


def load(ref, column):
    return [ref[pl.ds(column * 12 + 2 * part, 2)] for part in range(6)]


def store(ref, column, field):
    for part in range(6):
        ref[pl.ds(column * 12 + 2 * part, 2)] = field[part]


def prepare(field, links, inner, lower, partial_ref, below_ref, above_ref, column):
    partial = within(links, inner, field)
    turned = [swap_planes(a) for a in partial]
    store(partial_ref, column, partial)
    store(below_ref, column, [jnp.where(lower, f, t) for f, t in zip(field, turned)])
    store(above_ref, column, [jnp.where(lower, t, f) for f, t in zip(field, turned)])


def two_laplacians(partial, beyond, rim, links, inner, outer):
    single = product(link_at(outer, 0), beyond, False, partial)
    return single, product(link_at(outer, 0), rim, False, within(links, inner, single))


def arrived(from_below, from_above, lower):
    below, above = load(from_below, 0), load(from_above, 0)
    beyond = [swap_planes(jnp.where(lower, a, b)) for a, b in zip(above, below)]
    return beyond, [jnp.where(lower, b, a) for a, b in zip(above, below)]


def kernel_call(body, inputs, outputs, far=(), near=(), scratch=()):
    spec = pl.BlockSpec(memory_space=VMEM)
    spaces = [pltpu.HBM if at in far else pltpu.SMEM if at in near else VMEM for at in range(len(inputs))]
    inputs = [
        value if at in near else pltpu.with_memory_space_constraint(value, space)
        for at, (value, space) in enumerate(zip(inputs, spaces))
    ]
    shapes = [VMEM(shape, jnp.float32) for shape in outputs]
    return pl.pallas_call(
        body,
        in_specs=[pl.BlockSpec(memory_space=space) for space in spaces],
        out_specs=[spec] * len(outputs),
        out_shape=shapes,
        scratch_shapes=list(scratch),
        compiler_params=pltpu.CompilerParams(vmem_limit_bytes=32 * 1024 * 1024),
    )(*inputs)


FIELD = (12, 8, 128)
WITH_EDGE = (21, 8, 128)
WITH_RIM = (18, 8, 128)
CORE, HALF, TWIST = 0, 1, 2


def own_column(field, marks, message, base):
    half, twist = marks[HALF] > 0, marks[TWIST] > 0
    for part in range(6):
        for spin in range(2):
            low = jnp.where(twist, field[part, spin, 1], field[part, spin, 0])
            high = jnp.where(twist, field[part, spin, 3], field[part, spin, 2])
            message[base + part * 2 + spin] = jnp.where(half, high, low)


def pack_magnetic(magnetic, others):
    def raw(axis, imag, row, column):
        return magnetic[axis * 18 + imag * 9 + row * 3 + column]

    def real(axis, row, column):
        return 0.5 * (raw(axis, 0, row, column) + raw(axis, 0, column, row))

    def imag(axis, row, column):
        return 0.5 * (raw(axis, 1, row, column) - raw(axis, 1, column, row))

    for row in range(3):
        for column in range(3):
            at = LADDER + 3 * row + column
            others[at] = real(0, row, column) + imag(1, row, column)
            others[at + 9] = imag(0, row, column) - real(1, row, column)
        others[LEVEL + row] = real(2, row, row)
    for slot, (row, column) in enumerate(((0, 1), (0, 2), (1, 2))):
        others[LEVEL + 3 + slot] = real(2, row, column)
        others[LEVEL + 6 + slot] = imag(2, row, column)


def pack(space, time, magnetic, carried, own, field, raw, sems):
    copies = [
        pltpu.make_async_copy(source, target, sems.at[at])
        for at, (source, target) in enumerate(
            ((magnetic, raw), (space, own.at[pl.ds(0, 54)]), (time, own.at[pl.ds(54 + TIME, 18)]), (carried, field))
        )
    ]
    for copy in copies:
        copy.start()
    copies[0].wait()
    pack_magnetic(raw, own.at[pl.ds(54, 27)])
    for copy in copies[1:]:
        copy.wait()


def first_message(own, carried, marks, message):
    message[pl.ds(0, 54)] = own[pl.ds(0, 54)]
    own_column(carried, marks, message, 54)


def second_message(own, source, marks, message):
    message[pl.ds(0, 45)] = own[pl.ds(54, 45)]
    own_column(source, marks, message, 45)


def third_message(size, own, facing, message):
    message[pl.ds(0, size)] = own[pl.ds(0, size)]
    message[pl.ds(size, size)] = facing[...]


def pick(timeslice, own, facing, beside, marks, size, out):
    same_half = (marks[HALF] > 0) == (timeslice // 2 == 1)
    same_core = (marks[CORE] > 0) == (timeslice % 2 == 1)
    for at in range(size):
        mine = jnp.where(same_half, own[at], facing[at])
        theirs = jnp.where(same_half, beside[at], beside[size + at])
        out[at] = jnp.where(same_core, mine, theirs)


def arrange(links, inner, edge):
    first = rows_of((8, 128)) % 2 == 0
    turned = [swap_planes(links[at]) for at in range(18)]
    for row in range(3):
        for column in range(3):
            at, across = 3 * row + column, 3 * column + row
            inner[at] = jnp.where(first, links[at], turned[across])
            inner[at + 9] = jnp.where(first, links[at + 9], -turned[across + 9])
    for at in range(9):
        edge[at] = jnp.where(first, turned[at + 9], links[at])


def outgoing(from_below, links, outer):
    first = rows_of((8, 128)) % 2 == 0
    for row in range(3):
        for column in range(3):
            at, turned = 3 * row + column, 12 + 3 * column + row
            edge = from_below[turned]
            outer[at] = jnp.where(first, swap_planes(edge), links[at])
            outer[at + 9] = jnp.where(first, -edge, links[at + 9])


def begin(own, facing, beside, marks, field, links, inner, partial, to_below, to_above):
    pick(0, own, facing, beside, marks, 54, links)
    arrange(links, inner, to_above.at[pl.ds(12, 9)])
    lower = rows_of((8, 128)) % 2 == 0
    values = [own[pl.ds(54 + part * 2, 2)] for part in range(6)]
    store(field, 0, values)
    prepare(values, links, inner, lower, partial, to_below, to_above, 0)


def later_links(own, facing, beside, marks, *outs):
    for timeslice in range(1, SLICES):
        links, inner, edge = outs[3 * timeslice - 3 : 3 * timeslice]
        pick(timeslice, own, facing, beside, marks, 54, links)
        arrange(links, inner, edge)


def other_links(first, own, facing, beside, marks, *outs):
    for at, others in enumerate(outs):
        pick(first + at, own, facing, beside, marks, 45, others)


def aside(field, outer, others, base, back):
    values = load(field, 0)
    spin = spin_term(others, values)
    store(base, 0, [v + (0.5 * SPIN_WEIGHT) * b for v, b in zip(values, spin)])
    store(back, 0, product(link_at(outer, 0), values, True))


def step_a(base, back, partial, from_below, from_above, links, inner, outer, lower):
    beyond, rim = arrived(from_below, from_above, lower)
    single, double = two_laplacians(load(partial, 0), beyond, add(rim, load(back, 0)), links, inner, outer)
    return [
        f + (0.5 * KINETIC) * s + (0.5 * QUARTIC) * d for f, s, d in zip(load(base, 0), single, double)
    ]


def masked_sources(source_slice, others, marks, _, *outs):
    half, twist = marks[HALF] > 0, marks[TWIST] > 0
    for timeslice, out in enumerate(outs):
        on = [jnp.where(source_slice[column] == timeslice, 1.0, 0.0) for column in range(4)]
        weight = jnp.where(half, jnp.where(twist, on[3], on[2]), jnp.where(twist, on[1], on[0]))
        for at in range(12):
            out[at] = weight * others[45 + at]


def first_half(base, back, partial, from_below, from_above, links, inner, outer, others, *rest):
    rims, (turned_field, *messages) = rest[:-4], rest[-4:]
    lower = rows_of((8, 128)) % 2 == 0
    values = step_a(base, back, partial, from_below, from_above, links, inner, outer, lower)
    values = product(link_at(others, TIME), values, True)
    store(turned_field, 0, values)
    prepare(values, links, inner, lower, *messages, 0)
    for rim, message in zip(rims, messages[1:]):
        message[pl.ds(12, 6)] = rim[...]


def second_half(base, back, partial, from_below, from_above, links, inner, outer, source, *rest):
    lower = rows_of((8, 128)) % 2 == 0
    values = step_a(base, back, partial, from_below, from_above, links, inner, outer, lower)
    values = add(values, load(source, 0))
    if len(rest) == 4:
        result, *messages = rest
        store(result, 0, values)
        prepare(values, links, inner, lower, *messages, 0)
        return
    next_links, next_inner, next_edge, result, *messages = rest
    store(result, 0, values)
    prepare(values, next_links, next_inner, lower, *messages, 0)
    messages[2][pl.ds(12, 9)] = next_edge[...]


def smear_start(field, links, inner, partial_ref, rim_below, rim_above):
    first = rows_of((8, 128)) % 2 == 0
    partial = within(links, inner, load(field, 0))
    store(partial_ref, 0, partial)
    for part in range(6):
        up, down = partial[part][0], partial[part][1]
        rim_below[part] = jnp.where(first, up, swap_planes(down))
        rim_above[part] = jnp.where(first, swap_planes(up), down)


def smeared(field, partial, beyond, rim, links, inner, outer):
    rim = product(link_at(outer, 0), field, True, rim)
    single, double = two_laplacians(partial, beyond, rim, links, inner, outer)
    return [
        f + (2 * SMEAR_WEIGHT) * s + (SMEAR_WEIGHT * SMEAR_WEIGHT) * d
        for f, s, d in zip(field, single, double)
    ]


def smear_end(field, partial, from_below, from_above, rims_below, rims_above, links, inner, outer, out):
    lower = rows_of((8, 128)) % 2 == 0
    beyond = [
        swap_planes(jnp.where(lower, a, b)) for a, b in zip(load(from_above, 0), load(from_below, 0))
    ]
    rim = []
    for part in range(6):
        below, above = rims_below[12 + part], rims_above[12 + part]
        up = jnp.where(lower, below, swap_planes(above))
        down = jnp.where(lower, swap_planes(below), above)
        rim.append(jnp.stack([up, down]))
    store(out, 0, smeared(load(field, 0), load(partial, 0), beyond, rim, links, inner, outer))


def last_smear_end(field, partial, from_below, from_above, links, inner, outer, done_0, done_1, done_2, marks, mine, theirs):
    lower = rows_of((8, 128)) % 2 == 0
    core = marks[CORE] > 0
    below, above = load(from_below, 0), load(from_above, 0)
    beyond = [swap_planes(jnp.where(lower, a, b)) for a, b in zip(above, below)]
    rim = [jnp.where(lower, b, a) for a, b in zip(above, below)]
    last = smeared(load(field, 0), load(partial, 0), beyond, rim, links, inner, outer)
    for level, pair in enumerate(((load(done_0, 0), load(done_1, 0)), (load(done_2, 0), last))):
        store(mine, level, [jnp.where(core, b, a) for a, b in zip(*pair)])
        store(theirs, level, [jnp.where(core, a, b) for a, b in zip(*pair)])


def both_columns(way, mine, other, marks, *rest):
    half, twist = (marks[HALF] > 0) == (way == 0), marks[TWIST] > 0
    out = rest[-1]
    for at in range(12):
        own, beside = jnp.where(half, mine[12 + at], mine[at]), jnp.where(half, other[12 + at], other[at])
        out[at] = jnp.where(twist, beside, own)
        out[12 + at] = jnp.where(twist, own, beside)


def deliver(got0, got1, marks, out):
    half = marks[HALF] > 0
    for column in range(2):
        for part in range(6):
            for spin in range(2):
                at = column * 12 + part * 2 + spin
                out[part, spin, column] = jnp.where(half, got1[at], got0[at])
                out[part, spin, 2 + column] = jnp.where(half, got0[at], got1[at])


def registers(value, lead):
    rows = value.reshape(lead + (2, 4, 128))
    return jnp.swapaxes(rows, -3, -2).reshape(lead + (8, 128))


def exchange(to_below, to_above):
    return lax.ppermute(to_above, AXES, UP), lax.ppermute(to_below, AXES, DOWN)


def full(flag):
    return jnp.broadcast_to(flag.astype(jnp.float32), (8, 128))


def local(carried, source_field, source_slice, space_links, time_links, magnetic):
    section, space = lax.axis_index("section"), lax.axis_index("space")
    core, half = section % 2, section // 2
    x, y, z = space % 4, space // 4 % 4, space // 16
    twist_there = (core + x) % 2
    twist = (core + x + y + z) % 2
    marks_there = jnp.stack([full(core == 1), full(half == 1), full(twist_there == 1)])
    marks = jnp.stack([full(core == 1), full(half == 1), full(twist == 1)])

    carried = registers(carried, (6, 2, 4))
    source_field = registers(source_field, (6, 2, 4))
    space_links = registers(space_links, (54,))
    time_links = registers(time_links, (18,))
    magnetic = registers(magnetic, (54,))

    own, carried = kernel_call(
        pack,
        [space_links, time_links, magnetic, carried],
        [(99, 8, 128), (6, 2, 4, 8, 128)],
        far=range(4),
        scratch=[VMEM((54, 8, 128), jnp.float32), pltpu.SemaphoreType.DMA((4,))],
    )
    (message,) = kernel_call(first_message, [own, carried, marks_there], [(66, 8, 128)])
    links_own = lax.ppermute(message, AXES, SPREAD)
    (message,) = kernel_call(second_message, [own, source_field, marks_there], [(57, 8, 128)])
    others_own = lax.ppermute(message, AXES, SPREAD)
    links_facing = lax.ppermute(links_own[:54], AXES, FACING)
    others_facing = lax.ppermute(others_own[:45], AXES, FACING)
    (message,) = kernel_call(
        functools.partial(third_message, 54), [links_own, links_facing], [(108, 8, 128)]
    )
    links_beside = lax.ppermute(message, AXES, SIBLING)
    (message,) = kernel_call(
        functools.partial(third_message, 45), [others_own, others_facing], [(90, 8, 128)]
    )
    others_beside = lax.ppermute(message, AXES, SIBLING)

    field, links_0, inner_0, partial, to_below, to_above = kernel_call(
        begin,
        [links_own, links_facing, links_beside, marks],
        [FIELD, (54, 8, 128), (18, 8, 128), FIELD, FIELD, WITH_EDGE],
    )
    from_below, from_above = exchange(to_below, to_above)
    later = kernel_call(
        later_links,
        [links_own, links_facing, links_beside, marks],
        [(54, 8, 128), (18, 8, 128), (9, 8, 128)] * 3,
    )
    links, inner, edge = [links_0, *later[0::3]], [inner_0, *later[1::3]], [None, *later[2::3]]
    picked = [others_own, others_facing, others_beside, marks]
    others = kernel_call(functools.partial(other_links, 0), picked, [(45, 8, 128)])
    others += kernel_call(functools.partial(other_links, 1), picked, [(45, 8, 128)] * 3)

    sources = kernel_call(
        masked_sources, [source_slice, others_own, marks, to_below], [FIELD] * SLICES, near=(0,)
    )
    outer, done, rims = [], [], []
    for timeslice in range(SLICES):
        outer += kernel_call(outgoing, [from_below, links[timeslice]], [(18, 8, 128)])
        around = [links[timeslice], inner[timeslice], outer[timeslice], others[timeslice]]
        size = WITH_RIM if rims else FIELD
        before = [from_below, from_above]
        apart = kernel_call(aside, [field, outer[-1], others[timeslice]], [FIELD] * 2)
        field, partial, to_below, to_above = kernel_call(
            first_half, [*apart, partial, *before, *around, *rims], [FIELD, FIELD, size, size]
        )
        from_below, from_above = exchange(to_below, to_above)
        if rims:
            at = timeslice - 1
            done += kernel_call(
                smear_end,
                [result, smear_partial, *before, from_below, from_above, links[at], inner[at], outer[at]],
                [FIELD],
            )
        apart = kernel_call(aside, [field, outer[-1], others[timeslice]], [FIELD] * 2)
        inputs = [*apart, partial, from_below, from_above, *around[:3], sources[timeslice]]
        if timeslice + 1 < SLICES:
            after = [links[timeslice + 1], inner[timeslice + 1], edge[timeslice + 1]]
            field, partial, to_below, to_above = kernel_call(
                second_half, inputs + after, [FIELD, FIELD, FIELD, WITH_EDGE]
            )
            result = field
            smear_partial, *rims = kernel_call(
                smear_start, [field, links[timeslice], inner[timeslice]], [FIELD] + [(6, 8, 128)] * 2
            )
        else:
            field, partial, to_below, to_above = kernel_call(second_half, inputs, [FIELD] * 4)
        from_below, from_above = exchange(to_below, to_above)

    around = [links[-1], inner[-1], outer[-1]]
    mine, theirs = kernel_call(
        last_smear_end, [field, partial, from_below, from_above, *around, *done, marks], [(24, 8, 128)] * 2
    )
    other = lax.ppermute(theirs, AXES, SIBLING)
    (out1,) = kernel_call(functools.partial(both_columns, 1), [mine, other, marks], [(24, 8, 128)])
    got1 = lax.ppermute(out1, AXES, COLLECT[1])
    (out0,) = kernel_call(functools.partial(both_columns, 0), [mine, other, marks, out1], [(24, 8, 128)])
    got0 = lax.ppermute(out0, AXES, COLLECT[0])
    (out,) = kernel_call(deliver, [got0, got1, marks], [(6, 2, 4, 8, 128)])
    out = jnp.swapaxes(out.reshape(2, 3, 2, 4, 4, 2, 128), -3, -2)
    return out.reshape(1, 2, 3, 2, 4, 2, 512)


def solution(mesh):
    return jax.shard_map(
        local,
        mesh=mesh,
        in_specs=(
            P(None, None, None, None, "space", None),
            P(None, None, None, None, "space", None),
            P(),
            P("section", None, None, None, None, "space", None),
            P("section", None, None, None, "space", None),
            P("section", None, None, None, None, "space", None),
        ),
        out_specs=P("section", None, None, None, None, "space", None),
        check_vma=False,
    )
```

```python
import functools

import jax
import jax.numpy as jnp
from jax import lax
from jax.experimental import pallas as pl
from jax.experimental.pallas import tpu as pltpu
from jax.sharding import PartitionSpec as P


LZ = 16
KINETIC = 1.0 / 6.0
QUARTIC = 1.0 / 216.0
SPIN_WEIGHT = 1.0 / 6.0
SMEAR_WEIGHT = 0.1
AXES = ("section", "space")
VMEM = pltpu.VMEM
PAIRS = 32
SLICES = 4


def chip(pair):
    at = min(pair, PAIRS - 1 - pair)
    y, x = divmod(at, 4)
    return (x if y % 2 == 0 else 3 - x), y, pair // 16


def place(half, core, pair):
    x, y, z = chip(pair % PAIRS)
    return (2 * half + core) * 32 + z * 16 + y * 4 + x


def natural(half, core, pair):
    return (2 * half + core) * 32 + pair


EVERY = [(half, core, pair) for half in range(2) for core in range(2) for pair in range(PAIRS)]
SPREAD = [(natural(h, c, j), place(h, c, j)) for h, c, j in EVERY]
COLLECT = [[(place(h, c, j), natural(h ^ way, c, j)) for h, c, j in EVERY] for way in range(2)]
UP = [(place(h, c, j), place(h, 1 - c, j + 1)) for h, c, j in EVERY]
DOWN = [(place(h, c, j), place(h, 1 - c, j - 1)) for h, c, j in EVERY]
SIBLING = [(place(h, c, j), place(h, 1 - c, j)) for h, c, j in EVERY]
FACING = [(place(h, c, j), place(1 - h, c, j)) for h, c, j in EVERY]


def rows_of(shape):
    return lax.broadcasted_iota(jnp.int32, shape, len(shape) - 2)


def lanes_of(shape):
    return lax.broadcasted_iota(jnp.int32, shape, len(shape) - 1)


def roll(value, by, axis):
    return pltpu.roll(value, by, value.ndim + axis)


def swap_planes(value):
    first = rows_of(value.shape) % 2 == 0
    return jnp.where(first, roll(value, 7, -2), roll(value, 1, -2))


def y_forward(value):
    moved = roll(value, 112, -1)
    return jnp.where(lanes_of(value.shape) < 112, moved, roll(moved, 6, -2))


def y_backward(value):
    moved = roll(value, 16, -1)
    return jnp.where(lanes_of(value.shape) >= 16, moved, roll(moved, 2, -2))


def z_forward(value):
    inside = lanes_of(value.shape) % LZ < LZ - 1
    return jnp.where(inside, roll(value, 127, -1), roll(value, LZ - 1, -1))


def z_backward(value):
    inside = lanes_of(value.shape) % LZ > 0
    return jnp.where(inside, roll(value, 1, -1), roll(value, 129 - LZ, -1))


def add(one, other):
    return [a + b for a, b in zip(one, other)]


def scaled(factor, field):
    return [factor * a for a in field]


def link_at(ref, base):
    def entry(row, column):
        return ref[base + 3 * row + column], ref[base + 9 + 3 * row + column]

    return entry


def product(entry, field, dagger, total=None):
    real, imag = [], []
    for out in range(3):
        sum_real = None if total is None else total[out]
        sum_imag = None if total is None else total[3 + out]
        for inner in range(3):
            link_real, link_imag = entry(inner, out) if dagger else entry(out, inner)
            field_real, field_imag = field[inner], field[3 + inner]
            cross_real, cross_imag = link_imag * field_imag, link_imag * field_real
            part_real, part_imag = link_real * field_real, link_real * field_imag
            if dagger:
                part_real, part_imag = part_real + cross_real, part_imag - cross_imag
            else:
                part_real, part_imag = part_real - cross_real, part_imag + cross_imag
            sum_real = part_real if sum_real is None else sum_real + part_real
            sum_imag = part_imag if sum_imag is None else sum_imag + part_imag
        real.append(sum_real)
        imag.append(sum_imag)
    return real + imag


ALONG_X, ALONG_Y, ALONG_Z = 0, 18, 36


def within(links, inner, field):
    total = scaled(-6.0, field)
    total = product(link_at(links, ALONG_Y), [y_forward(a) for a in field], False, total)
    back = product(link_at(links, ALONG_Y), field, True)
    total = add(total, [y_backward(a) for a in back])
    total = product(link_at(links, ALONG_Z), [z_forward(a) for a in field], False, total)
    back = product(link_at(links, ALONG_Z), field, True)
    total = add(total, [z_backward(a) for a in back])
    return product(link_at(inner, 0), [swap_planes(a) for a in field], False, total)


LADDER, LEVEL, TIME = 0, 18, 27


def level_entry(ref):
    def entry(row, column):
        if row == column:
            return ref[LEVEL + row], None
        slot = min(row, column) + max(row, column) - 1
        imag = ref[LEVEL + 6 + slot]
        return ref[LEVEL + 3 + slot], imag if row < column else -imag

    return entry


def hermitian_product(entry, field):
    real, imag = [], []
    for out in range(3):
        sum_real = sum_imag = None
        for inner in range(3):
            link_real, link_imag = entry(out, inner)
            part_real, part_imag = link_real * field[inner], link_real * field[3 + inner]
            if link_imag is not None:
                part_real = part_real - link_imag * field[3 + inner]
                part_imag = part_imag + link_imag * field[inner]
            sum_real = part_real if sum_real is None else sum_real + part_real
            sum_imag = part_imag if sum_imag is None else sum_imag + part_imag
        real.append(sum_real)
        imag.append(sum_imag)
    return real + imag


def spin_term(others, field):
    up, down = [a[0] for a in field], [a[1] for a in field]
    ladder, level = link_at(others, LADDER), level_entry(others)
    upper = add(hermitian_product(level, up), product(ladder, down, False))
    lower = product(ladder, up, True)
    lower = [a - b for a, b in zip(lower, hermitian_product(level, down))]
    return [jnp.stack([a, b]) for a, b in zip(upper, lower)]


def load(ref, column):
    return [ref[pl.ds(column * 12 + 2 * part, 2)] for part in range(6)]


def store(ref, column, field):
    for part in range(6):
        ref[pl.ds(column * 12 + 2 * part, 2)] = field[part]


def prepare(field, links, inner, lower, partial_ref, below_ref, above_ref, column):
    partial = within(links, inner, field)
    turned = [swap_planes(a) for a in partial]
    store(partial_ref, column, partial)
    store(below_ref, column, [jnp.where(lower, f, t) for f, t in zip(field, turned)])
    store(above_ref, column, [jnp.where(lower, t, f) for f, t in zip(field, turned)])


def two_laplacians(partial, beyond, rim, links, inner, outer):
    single = product(link_at(outer, 0), beyond, False, partial)
    return single, product(link_at(outer, 0), rim, False, within(links, inner, single))


def arrived(from_below, from_above, lower):
    below, above = load(from_below, 0), load(from_above, 0)
    beyond = [swap_planes(jnp.where(lower, a, b)) for a, b in zip(above, below)]
    return beyond, [jnp.where(lower, b, a) for a, b in zip(above, below)]


def kernel_call(body, inputs, outputs, far=(), near=(), scratch=()):
    spec = pl.BlockSpec(memory_space=VMEM)
    spaces = [pltpu.HBM if at in far else pltpu.SMEM if at in near else VMEM for at in range(len(inputs))]
    inputs = [
        value if at in near else pltpu.with_memory_space_constraint(value, space)
        for at, (value, space) in enumerate(zip(inputs, spaces))
    ]
    shapes = [VMEM(shape, jnp.float32) for shape in outputs]
    return pl.pallas_call(
        body,
        in_specs=[pl.BlockSpec(memory_space=space) for space in spaces],
        out_specs=[spec] * len(outputs),
        out_shape=shapes,
        scratch_shapes=list(scratch),
        compiler_params=pltpu.CompilerParams(vmem_limit_bytes=32 * 1024 * 1024),
    )(*inputs)


FIELD = (12, 8, 128)
WITH_EDGE = (21, 8, 128)
WITH_RIM = (18, 8, 128)
CORE, HALF, TWIST = 0, 1, 2


def own_column(field, marks, message, base):
    half, twist = marks[HALF] > 0, marks[TWIST] > 0
    for part in range(6):
        for spin in range(2):
            low = jnp.where(twist, field[part, spin, 1], field[part, spin, 0])
            high = jnp.where(twist, field[part, spin, 3], field[part, spin, 2])
            message[base + part * 2 + spin] = jnp.where(half, high, low)


def pack_magnetic(magnetic, others):
    def raw(axis, imag, row, column):
        return magnetic[axis * 18 + imag * 9 + row * 3 + column]

    def real(axis, row, column):
        return 0.5 * (raw(axis, 0, row, column) + raw(axis, 0, column, row))

    def imag(axis, row, column):
        return 0.5 * (raw(axis, 1, row, column) - raw(axis, 1, column, row))

    for row in range(3):
        for column in range(3):
            at = LADDER + 3 * row + column
            others[at] = real(0, row, column) + imag(1, row, column)
            others[at + 9] = imag(0, row, column) - real(1, row, column)
        others[LEVEL + row] = real(2, row, row)
    for slot, (row, column) in enumerate(((0, 1), (0, 2), (1, 2))):
        others[LEVEL + 3 + slot] = real(2, row, column)
        others[LEVEL + 6 + slot] = imag(2, row, column)


def pack(space, time, magnetic, carried, own, field, raw, sems):
    copies = [
        pltpu.make_async_copy(source, target, sems.at[at])
        for at, (source, target) in enumerate(
            ((magnetic, raw), (space, own.at[pl.ds(0, 54)]), (time, own.at[pl.ds(54 + TIME, 18)]), (carried, field))
        )
    ]
    for copy in copies:
        copy.start()
    copies[0].wait()
    pack_magnetic(raw, own.at[pl.ds(54, 27)])
    for copy in copies[1:]:
        copy.wait()


def first_message(own, carried, marks, message):
    message[pl.ds(0, 54)] = own[pl.ds(0, 54)]
    own_column(carried, marks, message, 54)


def second_message(own, source, marks, message):
    message[pl.ds(0, 45)] = own[pl.ds(54, 45)]
    own_column(source, marks, message, 45)


def third_message(size, own, facing, message):
    message[pl.ds(0, size)] = own[pl.ds(0, size)]
    message[pl.ds(size, size)] = facing[...]


def pick(timeslice, own, facing, beside, marks, size, out):
    same_half = (marks[HALF] > 0) == (timeslice // 2 == 1)
    same_core = (marks[CORE] > 0) == (timeslice % 2 == 1)
    for at in range(size):
        mine = jnp.where(same_half, own[at], facing[at])
        theirs = jnp.where(same_half, beside[at], beside[size + at])
        out[at] = jnp.where(same_core, mine, theirs)


def arrange(links, inner, edge):
    first = rows_of((8, 128)) % 2 == 0
    turned = [swap_planes(links[at]) for at in range(18)]
    for row in range(3):
        for column in range(3):
            at, across = 3 * row + column, 3 * column + row
            inner[at] = jnp.where(first, links[at], turned[across])
            inner[at + 9] = jnp.where(first, links[at + 9], -turned[across + 9])
    for at in range(9):
        edge[at] = jnp.where(first, turned[at + 9], links[at])


def outgoing(from_below, links, outer):
    first = rows_of((8, 128)) % 2 == 0
    for row in range(3):
        for column in range(3):
            at, turned = 3 * row + column, 12 + 3 * column + row
            edge = from_below[turned]
            outer[at] = jnp.where(first, swap_planes(edge), links[at])
            outer[at + 9] = jnp.where(first, -edge, links[at + 9])


def begin(own, facing, beside, marks, field, links, inner, partial, to_below, to_above):
    pick(0, own, facing, beside, marks, 54, links)
    arrange(links, inner, to_above.at[pl.ds(12, 9)])
    lower = rows_of((8, 128)) % 2 == 0
    values = [own[pl.ds(54 + part * 2, 2)] for part in range(6)]
    store(field, 0, values)
    prepare(values, links, inner, lower, partial, to_below, to_above, 0)


def later_links(own, facing, beside, marks, *outs):
    for timeslice in range(1, SLICES):
        links, inner, edge = outs[3 * timeslice - 3 : 3 * timeslice]
        pick(timeslice, own, facing, beside, marks, 54, links)
        arrange(links, inner, edge)


def other_links(first, own, facing, beside, marks, *outs):
    for at, others in enumerate(outs):
        pick(first + at, own, facing, beside, marks, 45, others)


def aside(field, outer, others, base, back):
    values = load(field, 0)
    spin = spin_term(others, values)
    store(base, 0, [v + (0.5 * SPIN_WEIGHT) * b for v, b in zip(values, spin)])
    store(back, 0, product(link_at(outer, 0), values, True))


def step_a(base, back, partial, from_below, from_above, links, inner, outer, lower):
    beyond, rim = arrived(from_below, from_above, lower)
    single, double = two_laplacians(load(partial, 0), beyond, add(rim, load(back, 0)), links, inner, outer)
    return [
        f + (0.5 * KINETIC) * s + (0.5 * QUARTIC) * d for f, s, d in zip(load(base, 0), single, double)
    ]


def masked_sources(source_slice, others, marks, _, *outs):
    half, twist = marks[HALF] > 0, marks[TWIST] > 0
    for timeslice, out in enumerate(outs):
        on = [jnp.where(source_slice[column] == timeslice, 1.0, 0.0) for column in range(4)]
        weight = jnp.where(half, jnp.where(twist, on[3], on[2]), jnp.where(twist, on[1], on[0]))
        for at in range(12):
            out[at] = weight * others[45 + at]


def first_half(base, back, partial, from_below, from_above, links, inner, outer, others, *rest):
    rims, (turned_field, *messages) = rest[:-4], rest[-4:]
    lower = rows_of((8, 128)) % 2 == 0
    values = step_a(base, back, partial, from_below, from_above, links, inner, outer, lower)
    values = product(link_at(others, TIME), values, True)
    store(turned_field, 0, values)
    prepare(values, links, inner, lower, *messages, 0)
    for rim, message in zip(rims, messages[1:]):
        message[pl.ds(12, 6)] = rim[...]


def second_half(base, back, partial, from_below, from_above, links, inner, outer, source, *rest):
    lower = rows_of((8, 128)) % 2 == 0
    values = step_a(base, back, partial, from_below, from_above, links, inner, outer, lower)
    values = add(values, load(source, 0))
    if len(rest) == 4:
        result, *messages = rest
        store(result, 0, values)
        prepare(values, links, inner, lower, *messages, 0)
        return
    next_links, next_inner, next_edge, result, *messages = rest
    store(result, 0, values)
    prepare(values, next_links, next_inner, lower, *messages, 0)
    messages[2][pl.ds(12, 9)] = next_edge[...]


def smear_start(field, links, inner, partial_ref, rim_below, rim_above):
    first = rows_of((8, 128)) % 2 == 0
    partial = within(links, inner, load(field, 0))
    store(partial_ref, 0, partial)
    for part in range(6):
        up, down = partial[part][0], partial[part][1]
        rim_below[part] = jnp.where(first, up, swap_planes(down))
        rim_above[part] = jnp.where(first, swap_planes(up), down)


def smeared(field, partial, beyond, rim, links, inner, outer):
    rim = product(link_at(outer, 0), field, True, rim)
    single, double = two_laplacians(partial, beyond, rim, links, inner, outer)
    return [
        f + (2 * SMEAR_WEIGHT) * s + (SMEAR_WEIGHT * SMEAR_WEIGHT) * d
        for f, s, d in zip(field, single, double)
    ]


def smear_end(field, partial, from_below, from_above, rims_below, rims_above, links, inner, outer, out):
    lower = rows_of((8, 128)) % 2 == 0
    beyond = [
        swap_planes(jnp.where(lower, a, b)) for a, b in zip(load(from_above, 0), load(from_below, 0))
    ]
    rim = []
    for part in range(6):
        below, above = rims_below[12 + part], rims_above[12 + part]
        up = jnp.where(lower, below, swap_planes(above))
        down = jnp.where(lower, swap_planes(below), above)
        rim.append(jnp.stack([up, down]))
    store(out, 0, smeared(load(field, 0), load(partial, 0), beyond, rim, links, inner, outer))


def last_smear_end(field, partial, from_below, from_above, links, inner, outer, done_0, done_1, done_2, marks, mine, theirs):
    lower = rows_of((8, 128)) % 2 == 0
    core = marks[CORE] > 0
    below, above = load(from_below, 0), load(from_above, 0)
    beyond = [swap_planes(jnp.where(lower, a, b)) for a, b in zip(above, below)]
    rim = [jnp.where(lower, b, a) for a, b in zip(above, below)]
    last = smeared(load(field, 0), load(partial, 0), beyond, rim, links, inner, outer)
    for level, pair in enumerate(((load(done_0, 0), load(done_1, 0)), (load(done_2, 0), last))):
        store(mine, level, [jnp.where(core, b, a) for a, b in zip(*pair)])
        store(theirs, level, [jnp.where(core, a, b) for a, b in zip(*pair)])


def both_columns(way, mine, other, marks, *rest):
    half, twist = (marks[HALF] > 0) == (way == 0), marks[TWIST] > 0
    out = rest[-1]
    for at in range(12):
        own, beside = jnp.where(half, mine[12 + at], mine[at]), jnp.where(half, other[12 + at], other[at])
        out[at] = jnp.where(twist, beside, own)
        out[12 + at] = jnp.where(twist, own, beside)
    if way == 1:
        out[24] = marks[HALF]


def deliver(got0, got1, marks, out):
    half = marks[HALF] > 0
    for column in range(2):
        for part in range(6):
            for spin in range(2):
                at = column * 12 + part * 2 + spin
                out[part, spin, column] = jnp.where(half, got1[at], got0[at])
                out[part, spin, 2 + column] = jnp.where(half, got0[at], got1[at])


def registers(value, lead):
    rows = value.reshape(lead + (2, 4, 128))
    return jnp.swapaxes(rows, -3, -2).reshape(lead + (8, 128))


def exchange(to_below, to_above):
    return lax.ppermute(to_above, AXES, UP), lax.ppermute(to_below, AXES, DOWN)


def full(flag):
    return jnp.broadcast_to(flag.astype(jnp.float32), (8, 128))


def local(carried, source_field, source_slice, space_links, time_links, magnetic):
    section, space = lax.axis_index("section"), lax.axis_index("space")
    core, half = section % 2, section // 2
    x, y, z = space % 4, space // 4 % 4, space // 16
    twist_there = (core + x) % 2
    twist = (core + x + y + z) % 2
    marks_there = jnp.stack([full(core == 1), full(half == 1), full(twist_there == 1)])
    marks = jnp.stack([full(core == 1), full(half == 1), full(twist == 1)])

    carried = registers(carried, (6, 2, 4))
    source_field = registers(source_field, (6, 2, 4))
    space_links = registers(space_links, (54,))
    time_links = registers(time_links, (18,))
    magnetic = registers(magnetic, (54,))

    own, carried = kernel_call(
        pack,
        [space_links, time_links, magnetic, carried],
        [(99, 8, 128), (6, 2, 4, 8, 128)],
        far=range(4),
        scratch=[VMEM((54, 8, 128), jnp.float32), pltpu.SemaphoreType.DMA((4,))],
    )
    (message,) = kernel_call(first_message, [own, carried, marks_there], [(66, 8, 128)])
    links_own = lax.ppermute(message, AXES, SPREAD)
    (message,) = kernel_call(second_message, [own, source_field, marks_there], [(57, 8, 128)])
    others_own = lax.ppermute(message, AXES, SPREAD)
    links_facing = lax.ppermute(links_own[:54], AXES, FACING)
    others_facing = lax.ppermute(others_own[:45], AXES, FACING)
    (message,) = kernel_call(
        functools.partial(third_message, 54), [links_own, links_facing], [(108, 8, 128)]
    )
    links_beside = lax.ppermute(message, AXES, SIBLING)
    (message,) = kernel_call(
        functools.partial(third_message, 45), [others_own, others_facing], [(90, 8, 128)]
    )
    others_beside = lax.ppermute(message, AXES, SIBLING)

    field, links_0, inner_0, partial, to_below, to_above = kernel_call(
        begin,
        [links_own, links_facing, links_beside, marks],
        [FIELD, (54, 8, 128), (18, 8, 128), FIELD, FIELD, WITH_EDGE],
    )
    from_below, from_above = exchange(to_below, to_above)
    later = kernel_call(
        later_links,
        [links_own, links_facing, links_beside, marks],
        [(54, 8, 128), (18, 8, 128), (9, 8, 128)] * 3,
    )
    links, inner, edge = [links_0, *later[0::3]], [inner_0, *later[1::3]], [None, *later[2::3]]
    picked = [others_own, others_facing, others_beside, marks]
    others = kernel_call(functools.partial(other_links, 0), picked, [(45, 8, 128)])
    others += kernel_call(functools.partial(other_links, 1), picked, [(45, 8, 128)] * 3)

    sources = kernel_call(
        masked_sources, [source_slice, others_own, marks, to_below], [FIELD] * SLICES, near=(0,)
    )
    outer, done, rims = [], [], []
    for timeslice in range(SLICES):
        outer += kernel_call(outgoing, [from_below, links[timeslice]], [(18, 8, 128)])
        around = [links[timeslice], inner[timeslice], outer[timeslice], others[timeslice]]
        size = WITH_RIM if rims else FIELD
        before = [from_below, from_above]
        apart = kernel_call(aside, [field, outer[-1], others[timeslice]], [FIELD] * 2)
        field, partial, to_below, to_above = kernel_call(
            first_half, [*apart, partial, *before, *around, *rims], [FIELD, FIELD, size, size]
        )
        from_below, from_above = exchange(to_below, to_above)
        if rims:
            at = timeslice - 1
            done += kernel_call(
                smear_end,
                [result, smear_partial, *before, from_below, from_above, links[at], inner[at], outer[at]],
                [FIELD],
            )
        apart = kernel_call(aside, [field, outer[-1], others[timeslice]], [FIELD] * 2)
        inputs = [*apart, partial, from_below, from_above, *around[:3], sources[timeslice]]
        if timeslice + 1 < SLICES:
            after = [links[timeslice + 1], inner[timeslice + 1], edge[timeslice + 1]]
            field, partial, to_below, to_above = kernel_call(
                second_half, inputs + after, [FIELD, FIELD, FIELD, WITH_EDGE]
            )
            result = field
            smear_partial, *rims = kernel_call(
                smear_start, [field, links[timeslice], inner[timeslice]], [FIELD] + [(6, 8, 128)] * 2
            )
        else:
            field, partial, to_below, to_above = kernel_call(second_half, inputs, [FIELD] * 4)
        from_below, from_above = exchange(to_below, to_above)

    around = [links[-1], inner[-1], outer[-1]]
    mine, theirs = kernel_call(
        last_smear_end, [field, partial, from_below, from_above, *around, *done, marks], [(24, 8, 128)] * 2
    )
    other = lax.ppermute(theirs, AXES, SIBLING)
    (out1,) = kernel_call(functools.partial(both_columns, 1), [mine, other, marks], [(25, 8, 128)])
    got1 = lax.ppermute(out1, AXES, COLLECT[1])
    (out0,) = kernel_call(functools.partial(both_columns, 0), [mine, other, marks, out1], [(24, 8, 128)])
    got0 = lax.ppermute(out0, AXES, COLLECT[0])
    (out,) = kernel_call(deliver, [got0, got1, marks], [(6, 2, 4, 8, 128)])
    out = jnp.swapaxes(out.reshape(2, 3, 2, 4, 4, 2, 128), -3, -2)
    return out.reshape(1, 2, 3, 2, 4, 2, 512)


def solution(mesh):
    return jax.shard_map(
        local,
        mesh=mesh,
        in_specs=(
            P(None, None, None, None, "space", None),
            P(None, None, None, None, "space", None),
            P(),
            P("section", None, None, None, None, "space", None),
            P("section", None, None, None, "space", None),
            P("section", None, None, None, None, "space", None),
        ),
        out_specs=P("section", None, None, None, None, "space", None),
        check_vma=False,
    )
```

```python
import functools

import jax
import jax.numpy as jnp
from jax import lax
from jax.experimental import pallas as pl
from jax.experimental.pallas import tpu as pltpu
from jax.sharding import PartitionSpec as P


LZ = 16
KINETIC = 1.0 / 6.0
QUARTIC = 1.0 / 216.0
SPIN_WEIGHT = 1.0 / 6.0
SMEAR_WEIGHT = 0.1
AXES = ("section", "space")
VMEM = pltpu.VMEM
PAIRS = 32
SLICES = 4


def chip(pair):
    at = min(pair, PAIRS - 1 - pair)
    y, x = divmod(at, 4)
    return (x if y % 2 == 0 else 3 - x), y, pair // 16


def place(half, core, pair):
    x, y, z = chip(pair % PAIRS)
    return (2 * half + core) * 32 + z * 16 + y * 4 + x


def natural(half, core, pair):
    return (2 * half + core) * 32 + pair


EVERY = [(half, core, pair) for half in range(2) for core in range(2) for pair in range(PAIRS)]
SPREAD = [(natural(h, c, j), place(h, c, j)) for h, c, j in EVERY]
COLLECT = [[(place(h, c, j), natural(h ^ way, c, j)) for h, c, j in EVERY] for way in range(2)]
UP = [(place(h, c, j), place(h, 1 - c, j + 1)) for h, c, j in EVERY]
DOWN = [(place(h, c, j), place(h, 1 - c, j - 1)) for h, c, j in EVERY]
SIBLING = [(place(h, c, j), place(h, 1 - c, j)) for h, c, j in EVERY]
FACING = [(place(h, c, j), place(1 - h, c, j)) for h, c, j in EVERY]


def rows_of(shape):
    return lax.broadcasted_iota(jnp.int32, shape, len(shape) - 2)


def lanes_of(shape):
    return lax.broadcasted_iota(jnp.int32, shape, len(shape) - 1)


def roll(value, by, axis):
    return pltpu.roll(value, by, value.ndim + axis)


def swap_planes(value):
    first = rows_of(value.shape) % 2 == 0
    return jnp.where(first, roll(value, 7, -2), roll(value, 1, -2))


def y_forward(value):
    moved = roll(value, 112, -1)
    return jnp.where(lanes_of(value.shape) < 112, moved, roll(moved, 6, -2))


def y_backward(value):
    moved = roll(value, 16, -1)
    return jnp.where(lanes_of(value.shape) >= 16, moved, roll(moved, 2, -2))


def z_forward(value):
    inside = lanes_of(value.shape) % LZ < LZ - 1
    return jnp.where(inside, roll(value, 127, -1), roll(value, LZ - 1, -1))


def z_backward(value):
    inside = lanes_of(value.shape) % LZ > 0
    return jnp.where(inside, roll(value, 1, -1), roll(value, 129 - LZ, -1))


def add(one, other):
    return [a + b for a, b in zip(one, other)]


def scaled(factor, field):
    return [factor * a for a in field]


def link_at(ref, base):
    def entry(row, column):
        return ref[base + 3 * row + column], ref[base + 9 + 3 * row + column]

    return entry


def product(entry, field, dagger, total=None):
    real, imag = [], []
    for out in range(3):
        sum_real = None if total is None else total[out]
        sum_imag = None if total is None else total[3 + out]
        for inner in range(3):
            link_real, link_imag = entry(inner, out) if dagger else entry(out, inner)
            field_real, field_imag = field[inner], field[3 + inner]
            cross_real, cross_imag = link_imag * field_imag, link_imag * field_real
            part_real, part_imag = link_real * field_real, link_real * field_imag
            if dagger:
                part_real, part_imag = part_real + cross_real, part_imag - cross_imag
            else:
                part_real, part_imag = part_real - cross_real, part_imag + cross_imag
            sum_real = part_real if sum_real is None else sum_real + part_real
            sum_imag = part_imag if sum_imag is None else sum_imag + part_imag
        real.append(sum_real)
        imag.append(sum_imag)
    return real + imag


ALONG_X, ALONG_Y, ALONG_Z = 0, 18, 36


def within(links, inner, field):
    total = scaled(-6.0, field)
    total = product(link_at(links, ALONG_Y), [y_forward(a) for a in field], False, total)
    back = product(link_at(links, ALONG_Y), field, True)
    total = add(total, [y_backward(a) for a in back])
    total = product(link_at(links, ALONG_Z), [z_forward(a) for a in field], False, total)
    back = product(link_at(links, ALONG_Z), field, True)
    total = add(total, [z_backward(a) for a in back])
    return product(link_at(inner, 0), [swap_planes(a) for a in field], False, total)


LADDER, LEVEL, TIME = 0, 18, 27


def level_entry(ref):
    def entry(row, column):
        if row == column:
            return ref[LEVEL + row], None
        slot = min(row, column) + max(row, column) - 1
        imag = ref[LEVEL + 6 + slot]
        return ref[LEVEL + 3 + slot], imag if row < column else -imag

    return entry


def hermitian_product(entry, field):
    real, imag = [], []
    for out in range(3):
        sum_real = sum_imag = None
        for inner in range(3):
            link_real, link_imag = entry(out, inner)
            part_real, part_imag = link_real * field[inner], link_real * field[3 + inner]
            if link_imag is not None:
                part_real = part_real - link_imag * field[3 + inner]
                part_imag = part_imag + link_imag * field[inner]
            sum_real = part_real if sum_real is None else sum_real + part_real
            sum_imag = part_imag if sum_imag is None else sum_imag + part_imag
        real.append(sum_real)
        imag.append(sum_imag)
    return real + imag


def spin_term(others, field):
    up, down = [a[0] for a in field], [a[1] for a in field]
    ladder, level = link_at(others, LADDER), level_entry(others)
    upper = add(hermitian_product(level, up), product(ladder, down, False))
    lower = product(ladder, up, True)
    lower = [a - b for a, b in zip(lower, hermitian_product(level, down))]
    return [jnp.stack([a, b]) for a, b in zip(upper, lower)]


def load(ref, column):
    return [ref[pl.ds(column * 12 + 2 * part, 2)] for part in range(6)]


def store(ref, column, field):
    for part in range(6):
        ref[pl.ds(column * 12 + 2 * part, 2)] = field[part]


def prepare(field, links, inner, lower, partial_ref, below_ref, above_ref, column):
    partial = within(links, inner, field)
    turned = [swap_planes(a) for a in partial]
    store(partial_ref, column, partial)
    store(below_ref, column, [jnp.where(lower, f, t) for f, t in zip(field, turned)])
    store(above_ref, column, [jnp.where(lower, t, f) for f, t in zip(field, turned)])


def two_laplacians(partial, beyond, rim, links, inner, outer):
    single = product(link_at(outer, 0), beyond, False, partial)
    return single, product(link_at(outer, 0), rim, False, within(links, inner, single))


def arrived(from_below, from_above, lower):
    below, above = load(from_below, 0), load(from_above, 0)
    beyond = [swap_planes(jnp.where(lower, a, b)) for a, b in zip(above, below)]
    return beyond, [jnp.where(lower, b, a) for a, b in zip(above, below)]


def kernel_call(body, inputs, outputs, far=(), near=(), scratch=(), target=VMEM):
    spec = pl.BlockSpec(memory_space=target)
    spaces = [pltpu.HBM if at in far else pltpu.SMEM if at in near else VMEM for at in range(len(inputs))]
    inputs = [
        value if at in near else pltpu.with_memory_space_constraint(value, space)
        for at, (value, space) in enumerate(zip(inputs, spaces))
    ]
    shapes = [target(shape, jnp.float32) for shape in outputs]
    return pl.pallas_call(
        body,
        in_specs=[pl.BlockSpec(memory_space=space) for space in spaces],
        out_specs=[spec] * len(outputs),
        out_shape=shapes,
        scratch_shapes=list(scratch),
        compiler_params=pltpu.CompilerParams(vmem_limit_bytes=32 * 1024 * 1024),
    )(*inputs)


FIELD = (12, 8, 128)
WITH_EDGE = (21, 8, 128)
WITH_RIM = (18, 8, 128)
CORE, HALF, TWIST = 0, 1, 2


def own_column(field, marks, message, base):
    half, twist = marks[HALF] > 0, marks[TWIST] > 0
    for part in range(6):
        for spin in range(2):
            low = jnp.where(twist, field[part, spin, 1], field[part, spin, 0])
            high = jnp.where(twist, field[part, spin, 3], field[part, spin, 2])
            message[base + part * 2 + spin] = jnp.where(half, high, low)


def pack_magnetic(magnetic, others):
    def raw(axis, imag, row, column):
        return magnetic[axis * 18 + imag * 9 + row * 3 + column]

    def real(axis, row, column):
        return 0.5 * (raw(axis, 0, row, column) + raw(axis, 0, column, row))

    def imag(axis, row, column):
        return 0.5 * (raw(axis, 1, row, column) - raw(axis, 1, column, row))

    for row in range(3):
        for column in range(3):
            at = LADDER + 3 * row + column
            others[at] = real(0, row, column) + imag(1, row, column)
            others[at + 9] = imag(0, row, column) - real(1, row, column)
        others[LEVEL + row] = real(2, row, row)
    for slot, (row, column) in enumerate(((0, 1), (0, 2), (1, 2))):
        others[LEVEL + 3 + slot] = real(2, row, column)
        others[LEVEL + 6 + slot] = imag(2, row, column)


def pack(space, time, magnetic, carried, own, field, raw, sems):
    copies = [
        pltpu.make_async_copy(source, target, sems.at[at])
        for at, (source, target) in enumerate(
            ((magnetic, raw), (space, own.at[pl.ds(0, 54)]), (time, own.at[pl.ds(54 + TIME, 18)]), (carried, field))
        )
    ]
    for copy in copies:
        copy.start()
    copies[0].wait()
    pack_magnetic(raw, own.at[pl.ds(54, 27)])
    for copy in copies[1:]:
        copy.wait()


def first_message(own, carried, marks, message):
    message[pl.ds(0, 54)] = own[pl.ds(0, 54)]
    own_column(carried, marks, message, 54)


def second_message(own, source, marks, message):
    message[pl.ds(0, 45)] = own[pl.ds(54, 45)]
    own_column(source, marks, message, 45)


def third_message(size, own, facing, message):
    message[pl.ds(0, size)] = own[pl.ds(0, size)]
    message[pl.ds(size, size)] = facing[...]


def pick(timeslice, own, facing, beside, marks, size, out):
    same_half = (marks[HALF] > 0) == (timeslice // 2 == 1)
    same_core = (marks[CORE] > 0) == (timeslice % 2 == 1)
    for at in range(size):
        mine = jnp.where(same_half, own[at], facing[at])
        theirs = jnp.where(same_half, beside[at], beside[size + at])
        out[at] = jnp.where(same_core, mine, theirs)


def arrange(links, inner, edge):
    first = rows_of((8, 128)) % 2 == 0
    turned = [swap_planes(links[at]) for at in range(18)]
    for row in range(3):
        for column in range(3):
            at, across = 3 * row + column, 3 * column + row
            inner[at] = jnp.where(first, links[at], turned[across])
            inner[at + 9] = jnp.where(first, links[at + 9], -turned[across + 9])
    for at in range(9):
        edge[at] = jnp.where(first, turned[at + 9], links[at])


def outgoing(from_below, links, outer):
    first = rows_of((8, 128)) % 2 == 0
    for row in range(3):
        for column in range(3):
            at, turned = 3 * row + column, 12 + 3 * column + row
            edge = from_below[turned]
            outer[at] = jnp.where(first, swap_planes(edge), links[at])
            outer[at + 9] = jnp.where(first, -edge, links[at + 9])


def begin(own, facing, beside, marks, field, links, inner, partial, to_below, to_above):
    pick(0, own, facing, beside, marks, 54, links)
    arrange(links, inner, to_above.at[pl.ds(12, 9)])
    lower = rows_of((8, 128)) % 2 == 0
    values = [own[pl.ds(54 + part * 2, 2)] for part in range(6)]
    store(field, 0, values)
    prepare(values, links, inner, lower, partial, to_below, to_above, 0)


def later_links(own, facing, beside, marks, *outs):
    for timeslice in range(1, SLICES):
        links, inner, edge = outs[3 * timeslice - 3 : 3 * timeslice]
        pick(timeslice, own, facing, beside, marks, 54, links)
        arrange(links, inner, edge)


def other_links(first, own, facing, beside, marks, *outs):
    for at, others in enumerate(outs):
        pick(first + at, own, facing, beside, marks, 45, others)


def aside(field, outer, others, base, back):
    values = load(field, 0)
    spin = spin_term(others, values)
    store(base, 0, [v + (0.5 * SPIN_WEIGHT) * b for v, b in zip(values, spin)])
    store(back, 0, product(link_at(outer, 0), values, True))


def step_a(base, back, partial, from_below, from_above, links, inner, outer, lower):
    beyond, rim = arrived(from_below, from_above, lower)
    single, double = two_laplacians(load(partial, 0), beyond, add(rim, load(back, 0)), links, inner, outer)
    return [
        f + (0.5 * KINETIC) * s + (0.5 * QUARTIC) * d for f, s, d in zip(load(base, 0), single, double)
    ]


def masked_sources(source_slice, others, marks, _, *outs):
    half, twist = marks[HALF] > 0, marks[TWIST] > 0
    for timeslice, out in enumerate(outs):
        on = [jnp.where(source_slice[column] == timeslice, 1.0, 0.0) for column in range(4)]
        weight = jnp.where(half, jnp.where(twist, on[3], on[2]), jnp.where(twist, on[1], on[0]))
        for at in range(12):
            out[at] = weight * others[45 + at]


def first_half(base, back, partial, from_below, from_above, links, inner, outer, others, *rest):
    rims, (turned_field, *messages) = rest[:-4], rest[-4:]
    lower = rows_of((8, 128)) % 2 == 0
    values = step_a(base, back, partial, from_below, from_above, links, inner, outer, lower)
    values = product(link_at(others, TIME), values, True)
    store(turned_field, 0, values)
    prepare(values, links, inner, lower, *messages, 0)
    for rim, message in zip(rims, messages[1:]):
        message[pl.ds(12, 6)] = rim[...]


def second_half(base, back, partial, from_below, from_above, links, inner, outer, source, *rest):
    lower = rows_of((8, 128)) % 2 == 0
    values = step_a(base, back, partial, from_below, from_above, links, inner, outer, lower)
    values = add(values, load(source, 0))
    if len(rest) == 4:
        result, *messages = rest
        store(result, 0, values)
        prepare(values, links, inner, lower, *messages, 0)
        return
    next_links, next_inner, next_edge, result, *messages = rest
    store(result, 0, values)
    prepare(values, next_links, next_inner, lower, *messages, 0)
    messages[2][pl.ds(12, 9)] = next_edge[...]


def smear_start(field, links, inner, partial_ref, rim_below, rim_above):
    first = rows_of((8, 128)) % 2 == 0
    partial = within(links, inner, load(field, 0))
    store(partial_ref, 0, partial)
    for part in range(6):
        up, down = partial[part][0], partial[part][1]
        rim_below[part] = jnp.where(first, up, swap_planes(down))
        rim_above[part] = jnp.where(first, swap_planes(up), down)


def smeared(field, partial, beyond, rim, links, inner, outer):
    rim = product(link_at(outer, 0), field, True, rim)
    single, double = two_laplacians(partial, beyond, rim, links, inner, outer)
    return [
        f + (2 * SMEAR_WEIGHT) * s + (SMEAR_WEIGHT * SMEAR_WEIGHT) * d
        for f, s, d in zip(field, single, double)
    ]


def smear_end(field, partial, from_below, from_above, rims_below, rims_above, links, inner, outer, out):
    lower = rows_of((8, 128)) % 2 == 0
    beyond = [
        swap_planes(jnp.where(lower, a, b)) for a, b in zip(load(from_above, 0), load(from_below, 0))
    ]
    rim = []
    for part in range(6):
        below, above = rims_below[12 + part], rims_above[12 + part]
        up = jnp.where(lower, below, swap_planes(above))
        down = jnp.where(lower, swap_planes(below), above)
        rim.append(jnp.stack([up, down]))
    store(out, 0, smeared(load(field, 0), load(partial, 0), beyond, rim, links, inner, outer))


def last_smear_end(field, partial, from_below, from_above, links, inner, outer, done_0, done_1, done_2, marks, mine, theirs):
    lower = rows_of((8, 128)) % 2 == 0
    core = marks[CORE] > 0
    below, above = load(from_below, 0), load(from_above, 0)
    beyond = [swap_planes(jnp.where(lower, a, b)) for a, b in zip(above, below)]
    rim = [jnp.where(lower, b, a) for a, b in zip(above, below)]
    last = smeared(load(field, 0), load(partial, 0), beyond, rim, links, inner, outer)
    for level, pair in enumerate(((load(done_0, 0), load(done_1, 0)), (load(done_2, 0), last))):
        store(mine, level, [jnp.where(core, b, a) for a, b in zip(*pair)])
        store(theirs, level, [jnp.where(core, a, b) for a, b in zip(*pair)])


def both_columns(way, mine, other, marks, *rest):
    half, twist = (marks[HALF] > 0) == (way == 0), marks[TWIST] > 0
    out = rest[-1]
    for at in range(12):
        own, beside = jnp.where(half, mine[12 + at], mine[at]), jnp.where(half, other[12 + at], other[at])
        out[at] = jnp.where(twist, beside, own)
        out[12 + at] = jnp.where(twist, own, beside)
    if way == 1:
        out[24] = marks[HALF]


def deliver(got0, got1, marks, out, held, sems):
    half = marks[HALF] > 0
    copies = []
    for part in range(6):
        for column in range(2):
            for spin in range(2):
                at = column * 12 + part * 2 + spin
                held[part, spin, column] = jnp.where(half, got1[at], got0[at])
                held[part, spin, 2 + column] = jnp.where(half, got0[at], got1[at])
        copies.append(pltpu.make_async_copy(held.at[part], out.at[part], sems.at[part]))
        copies[-1].start()
    for copy in copies:
        copy.wait()


def registers(value, lead):
    rows = value.reshape(lead + (2, 4, 128))
    return jnp.swapaxes(rows, -3, -2).reshape(lead + (8, 128))


def exchange(to_below, to_above):
    return lax.ppermute(to_above, AXES, UP), lax.ppermute(to_below, AXES, DOWN)


def full(flag):
    return jnp.broadcast_to(flag.astype(jnp.float32), (8, 128))


def local(carried, source_field, source_slice, space_links, time_links, magnetic):
    section, space = lax.axis_index("section"), lax.axis_index("space")
    core, half = section % 2, section // 2
    x, y, z = space % 4, space // 4 % 4, space // 16
    twist_there = (core + x) % 2
    twist = (core + x + y + z) % 2
    marks_there = jnp.stack([full(core == 1), full(half == 1), full(twist_there == 1)])
    marks = jnp.stack([full(core == 1), full(half == 1), full(twist == 1)])

    carried = registers(carried, (6, 2, 4))
    source_field = registers(source_field, (6, 2, 4))
    space_links = registers(space_links, (54,))
    time_links = registers(time_links, (18,))
    magnetic = registers(magnetic, (54,))

    own, carried = kernel_call(
        pack,
        [space_links, time_links, magnetic, carried],
        [(99, 8, 128), (6, 2, 4, 8, 128)],
        far=range(4),
        scratch=[VMEM((54, 8, 128), jnp.float32), pltpu.SemaphoreType.DMA((4,))],
    )
    (message,) = kernel_call(first_message, [own, carried, marks_there], [(66, 8, 128)])
    links_own = lax.ppermute(message, AXES, SPREAD)
    (message,) = kernel_call(second_message, [own, source_field, marks_there], [(57, 8, 128)])
    others_own = lax.ppermute(message, AXES, SPREAD)
    links_facing = lax.ppermute(links_own[:54], AXES, FACING)
    others_facing = lax.ppermute(others_own[:45], AXES, FACING)
    (message,) = kernel_call(
        functools.partial(third_message, 54), [links_own, links_facing], [(108, 8, 128)]
    )
    links_beside = lax.ppermute(message, AXES, SIBLING)
    (message,) = kernel_call(
        functools.partial(third_message, 45), [others_own, others_facing], [(90, 8, 128)]
    )
    others_beside = lax.ppermute(message, AXES, SIBLING)

    field, links_0, inner_0, partial, to_below, to_above = kernel_call(
        begin,
        [links_own, links_facing, links_beside, marks],
        [FIELD, (54, 8, 128), (18, 8, 128), FIELD, FIELD, WITH_EDGE],
    )
    from_below, from_above = exchange(to_below, to_above)
    later = kernel_call(
        later_links,
        [links_own, links_facing, links_beside, marks],
        [(54, 8, 128), (18, 8, 128), (9, 8, 128)] * 3,
    )
    links, inner, edge = [links_0, *later[0::3]], [inner_0, *later[1::3]], [None, *later[2::3]]
    picked = [others_own, others_facing, others_beside, marks]
    others = kernel_call(functools.partial(other_links, 0), picked, [(45, 8, 128)])
    others += kernel_call(functools.partial(other_links, 1), picked, [(45, 8, 128)] * 3)

    sources = kernel_call(
        masked_sources, [source_slice, others_own, marks, to_below], [FIELD] * SLICES, near=(0,)
    )
    outer, done, rims = [], [], []
    for timeslice in range(SLICES):
        outer += kernel_call(outgoing, [from_below, links[timeslice]], [(18, 8, 128)])
        around = [links[timeslice], inner[timeslice], outer[timeslice], others[timeslice]]
        size = WITH_RIM if rims else FIELD
        before = [from_below, from_above]
        apart = kernel_call(aside, [field, outer[-1], others[timeslice]], [FIELD] * 2)
        field, partial, to_below, to_above = kernel_call(
            first_half, [*apart, partial, *before, *around, *rims], [FIELD, FIELD, size, size]
        )
        from_below, from_above = exchange(to_below, to_above)
        if rims:
            at = timeslice - 1
            done += kernel_call(
                smear_end,
                [result, smear_partial, *before, from_below, from_above, links[at], inner[at], outer[at]],
                [FIELD],
            )
        apart = kernel_call(aside, [field, outer[-1], others[timeslice]], [FIELD] * 2)
        inputs = [*apart, partial, from_below, from_above, *around[:3], sources[timeslice]]
        if timeslice + 1 < SLICES:
            after = [links[timeslice + 1], inner[timeslice + 1], edge[timeslice + 1]]
            field, partial, to_below, to_above = kernel_call(
                second_half, inputs + after, [FIELD, FIELD, FIELD, WITH_EDGE]
            )
            result = field
            smear_partial, *rims = kernel_call(
                smear_start, [field, links[timeslice], inner[timeslice]], [FIELD] + [(6, 8, 128)] * 2
            )
        else:
            field, partial, to_below, to_above = kernel_call(second_half, inputs, [FIELD] * 4)
        from_below, from_above = exchange(to_below, to_above)

    around = [links[-1], inner[-1], outer[-1]]
    mine, theirs = kernel_call(
        last_smear_end, [field, partial, from_below, from_above, *around, *done, marks], [(24, 8, 128)] * 2
    )
    other = lax.ppermute(theirs, AXES, SIBLING)
    (out1,) = kernel_call(functools.partial(both_columns, 1), [mine, other, marks], [(25, 8, 128)])
    got1 = lax.ppermute(out1, AXES, COLLECT[1])
    (out0,) = kernel_call(functools.partial(both_columns, 0), [mine, other, marks, out1], [(24, 8, 128)])
    got0 = lax.ppermute(out0, AXES, COLLECT[0])
    whole = (6, 2, 4, 8, 128)
    (out,) = kernel_call(
        deliver,
        [got0, got1, marks],
        [whole],
        scratch=[VMEM(whole, jnp.float32), pltpu.SemaphoreType.DMA((6,))],
        target=pltpu.HBM,
    )
    out = jnp.swapaxes(out.reshape(2, 3, 2, 4, 4, 2, 128), -3, -2)
    return out.reshape(1, 2, 3, 2, 4, 2, 512)


def solution(mesh):
    return jax.shard_map(
        local,
        mesh=mesh,
        in_specs=(
            P(None, None, None, None, "space", None),
            P(None, None, None, None, "space", None),
            P(),
            P("section", None, None, None, None, "space", None),
            P("section", None, None, None, "space", None),
            P("section", None, None, None, None, "space", None),
        ),
        out_specs=P("section", None, None, None, None, "space", None),
        check_vma=False,
    )
```
